32 devices in a mesh: node: 16 (over z, x, core), local: 2 (over y).
Axes of the slice: x: 2, y: 2, z: 4, core: 2. Of those that a mesh axis runs over, the one named last changes fastest.
Arguments:
- tokens: bfloat16 [256, 4096], P('node', 'local'), may hold values from -6 to 6
- grad_out: bfloat16 [256, 4096], P('node', 'local'), may hold values from -6 to 6
- gates: float32 [256, 8], P('node'), may hold values from 0.1 to 1
- expert_ids: int32 [256, 8], P('node'), may hold values from 0 to 15, all different within a row; in each aligned block of 16 rows (0 to 15, 16 to 31, ...) at most 16 rows name the same one
- w_gate: bfloat16 [16, 4096, 1024], P('node', 'local'), may hold values from -0.09375 to 0.09375
- w_up: bfloat16 [16, 4096, 1024], P('node', 'local'), may hold values from -0.09375 to 0.09375
- w_down: bfloat16 [16, 1024, 4096], P('node', None, 'local'), may hold values from -0.046875 to 0.046875
Outputs:
- grad_tokens: bfloat16 [256, 4096], P('node', 'local')
- grad_gates: bfloat16 [256, 8], P('node')
The draws below stay inside these ranges and needn't reach their ends.
Inputs may be any that keep to these rules, and one draw needn't show every extreme that they name: `expert_ids`: each row names 8 different experts. Among the 16 rows of one node rank no expert is named by more than 16 rows, a bound that some block reaches.
All inputs are finite; a program needn't handle non-finite values.
Results may differ from the reference program's by a relative error of at most 0.0057.
Values may be sent and summed in bfloat16 or wider, within the bound.
A program may use at most 64 MiB of HBM per device.

```python
import math
import jax
import jax.numpy as jnp
import numpy as np
from jax import lax

D = 4096
FF = 1024
TOPK = 8
TOK_NODE = 16
EXPERTS = 16
CAP = 16
TOKENS = 256
N_NODE = 16


def block_scale(own_key, dims, split, smallest, top_value):
    factor_of, own = 1.0, jax.random.fold_in(own_key, 6)
    for dim, shards_of in split:
        draws = jnp.exp(jax.random.uniform(jax.random.fold_in(own, dim), (shards_of,), jnp.float32, smallest / len(split), top_value / len(split)))
        factor_of = factor_of * jnp.repeat(draws, dims[dim] // shards_of).reshape([-1 if axis == dim else 1 for axis in range(len(dims))])
    return factor_of


def deal_out(rng, own, number, rows, count, top, bound, skew):
    order = jax.random.permutation(rng, count)
    packed, common = portions_of(count, rows * top, bound, skew, True), portions_of(count, rows * top, bound, skew, False)
    places = jnp.arange(count)

    def named(tallies, offset_by):
        used = int((tallies > 0).sum())
        fixed = max(1, used // 4)
        moved = fixed + (places - fixed + offset_by * (used - fixed)) % max(1, count - fixed)
        return jnp.zeros((count,), jnp.int32).at[order[jnp.where(places < fixed, places, moved)]].set(jnp.asarray(tallies, jnp.int32))

    tallies = jnp.where(number % 4 == 0, named(packed, number // 4), named(common, number - number // 4 - 1))
    mixed = jax.random.permutation(jax.random.fold_in(own, 3), count)
    source_of, taker = mixed[0:count // 2 * 2:2], mixed[1:count // 2 * 2:2]
    slack = jnp.minimum(tallies[source_of] - 1, bound - tallies[taker]) // 2
    slack = jnp.where((source_of == order[0]) | (taker == order[0]) | (tallies[taker] == 0), 0, jnp.maximum(slack, 0))
    moved = jax.random.randint(jax.random.fold_in(own, 4), (count // 2,), 0, 1 << 20) % (slack + 1)
    tallies = tallies.at[source_of].add(-moved).at[taker].add(moved)
    labels = jnp.searchsorted(jnp.cumsum(tallies), jnp.arange(rows * top), side="right").astype(jnp.int32)
    grid = labels.reshape(top, rows).T
    grid = grid[jax.random.permutation(jax.random.fold_in(own, 1), rows)]
    offset_by = jax.random.randint(jax.random.fold_in(own, 2), (rows, 1), 0, top)
    return jnp.take_along_axis(grid, (jnp.arange(top)[None, :] + offset_by) % top, axis=1)


def portions_of(count, total, limit, slope, full):
    portions = [(1 << 20) // math.isqrt(rank ** slope) + 1 for rank in range(1, count + 1)]
    largest = limit if full else min(limit, max(-(-total // count), total * portions[0] // sum(portions)))
    least = 1 if total - largest >= count - 1 else 0
    holding, spare = [largest] + [least] * (count - 1), total - largest - least * (count - 1)
    while spare > 0:
        free = [i for i in range(1, count) if holding[i] < largest] or [i for i in range(1, count) if holding[i] < limit]
        mass, remaining = sum([portions[i] for i in free]), spare
        for i in free:
            extra = min(limit - holding[i], max(1, remaining * portions[i] // mass), spare)
            holding[i] = holding[i] + extra
            spare = spare - extra
    return np.array(holding)


def centred(rng, dims, width, bound, shards=(), held_as=jnp.bfloat16):
    entries = width * jax.random.normal(rng, dims, jnp.float32)
    if shards:
        entries = entries * block_scale(rng, dims, shards, -0.22, 0.18)
    return jnp.clip(entries, -bound, bound).astype(held_as)


def setup_inputs(seed: int = 0) -> dict:
    key_of = jax.random.split(jax.random.key(seed), 8)
    tokens = centred(key_of[0], (TOKENS, D), 1.0, 6.0, ((0, 16), (1, 2)))
    grad_out = centred(key_of[1], (TOKENS, D), 1.0, 6.0, ((0, 16), (1, 2)))
    gates = jnp.clip(jnp.exp(math.log(1.0) - 2.3025851 * jax.random.uniform(key_of[2], (TOKENS, TOPK), jnp.float32) ** block_scale(key_of[2], (TOKENS, TOPK), ((0, 16),), -0.2, 0.2)), 0.1, 1.0)
    expert_ids_keys = jax.random.split(jax.random.fold_in(key_of[3], 1), TOKENS // TOK_NODE)
    expert_ids_turns = jax.random.permutation(jax.random.fold_in(key_of[3], 3), TOKENS // TOK_NODE)
    expert_ids = jax.vmap(lambda own, number: deal_out(jax.random.fold_in(key_of[3], 2), own, number, TOK_NODE, EXPERTS, TOPK, CAP, 2))(expert_ids_keys, expert_ids_turns).reshape((TOKENS, TOPK))
    w_gate = centred(key_of[4], (EXPERTS, D, FF), D ** -0.5, 0.09375, ((0, 16), (1, 2)))
    w_up = centred(key_of[5], (EXPERTS, D, FF), D ** -0.5, 0.09375, ((0, 16), (1, 2)))
    w_down = centred(key_of[6], (EXPERTS, FF, D), (16 * FF) ** -0.5, 0.046875, ((0, 16), (2, 2)))
    return dict(tokens=tokens, grad_out=grad_out, gates=gates, expert_ids=expert_ids, w_gate=w_gate, w_up=w_up, w_down=w_down)


def node_slots(expert_ids):
    grouped = expert_ids.reshape(N_NODE, TOK_NODE * TOPK).astype(jnp.int32)
    onehot = (grouped[:, :, None] == jnp.arange(EXPERTS, dtype=jnp.int32)[None, None, :]).astype(jnp.int32)
    slot_rank = jnp.sum(onehot * (jnp.cumsum(onehot, axis=1) - 1), axis=2)
    return grouped, slot_rank.astype(jnp.int32)


def reference(tokens, grad_out, gates, expert_ids, w_gate, w_up, w_down):
    grouped, slot_rank = node_slots(expert_ids)
    source = jnp.broadcast_to(jnp.arange(N_NODE, dtype=jnp.int32)[:, None], grouped.shape)
    position = (source * CAP + slot_rank).reshape(-1).astype(jnp.int32)
    owner = grouped.reshape(-1).astype(jnp.int32)
    pair_index = jnp.arange(TOKENS * TOPK, dtype=jnp.int32)
    slot_table = jnp.zeros((EXPERTS, N_NODE * CAP), jnp.int32).at[owner, position].set(pair_index)
    slot_valid = jnp.zeros((EXPERTS, N_NODE * CAP), jnp.float32).at[owner, position].set(1.0)
    gate_flat = gates.reshape(-1)

    def expert_step(running, expert):
        grad_sum, gate_grads = running
        pairs = slot_table[expert]
        token_index = (pairs // TOPK).astype(jnp.int32)
        valid = slot_valid[expert]
        x_rows = jnp.take(tokens, token_index, axis=0)
        dy_rows = jnp.take(grad_out, token_index, axis=0)
        gate_pre = jnp.dot(x_rows, w_gate[expert], preferred_element_type=jnp.float32)
        up_pre = jnp.dot(x_rows, w_up[expert], preferred_element_type=jnp.float32)
        back_pre = lax.dot_general(dy_rows, w_down[expert], (((1,), (1,)), ((), ())), preferred_element_type=jnp.float32)
        sigmoid_gate = jax.nn.sigmoid(gate_pre)
        act = gate_pre * sigmoid_gate
        gate_part = jnp.sum(act * up_pre * back_pre, axis=1).astype(jnp.bfloat16)
        grad_up = (back_pre * act).astype(jnp.bfloat16)
        grad_gate = (back_pre * up_pre * sigmoid_gate * (1.0 + gate_pre * (1.0 - sigmoid_gate))).astype(jnp.bfloat16)
        row_grads = lax.dot_general(grad_gate, w_gate[expert], (((1,), (1,)), ((), ())), preferred_element_type=jnp.float32)
        row_grads = row_grads + lax.dot_general(grad_up, w_up[expert], (((1,), (1,)), ((), ())), preferred_element_type=jnp.float32)
        row_grads = row_grads.astype(jnp.bfloat16)
        weight = jnp.take(gate_flat, pairs) * valid
        grad_sum = grad_sum.at[token_index].add(weight[:, None] * row_grads.astype(jnp.float32))
        gate_grads = gate_grads.at[pairs].add(valid * gate_part.astype(jnp.float32))
        return (grad_sum, gate_grads), None

    start_state = (jnp.zeros((TOKENS, D), jnp.float32), jnp.zeros((TOKENS * TOPK,), jnp.float32))
    final, unused = lax.scan(expert_step, start_state, jnp.arange(EXPERTS, dtype=jnp.int32))
    grad_sum, gate_grads = final
    return grad_sum.astype(jnp.bfloat16), gate_grads.reshape(TOKENS, TOPK).astype(jnp.bfloat16)
```

```python
import functools

import jax
import jax.numpy as jnp
from jax import lax
from jax.experimental import pallas as pl
from jax.experimental.pallas import tpu as pltpu
from jax.sharding import PartitionSpec as P

MESH = pl.DeviceIdType.MESH
LANES = 128
TILE = 256
AG_Z, AG_X, AG_A, AG_B, SUM_Y, GRAD_Y, RS_C, RS_X, RS_Z, KINDS = 0, 1, 2, 3, 4, 7, 8, 9, 10, 11
NT = (((1,), (1,)), ((), ()))


def flipped(value, bits):
    place = 1
    while place <= bits:
        if bits & place:
            value = value + place * (1 - 2 * lax.rem(lax.div(value, place), 2))
        place *= 2
    return value


def dense_kernel(
    planes, tokens, grad_out, gates, ids, wg_hbm, wu_hbm, wd_hbm, out, out_gates,
    wg, wu, wd, gath, part, sum_send, sum_recv, grads, pair, rc_send, rc_recv,
    rx_send, rx_recv, rz_send, rz_recv, w_sem, send_sem, recv_sem,
):
    node, y = lax.axis_index("node"), lax.axis_index("local")
    core, x, z = lax.rem(node, 2), lax.rem(lax.div(node, 2), 2), lax.div(node, 4)
    rows, feat = tokens.shape
    hidden = wg.shape[1]
    experts = 4 * planes
    half = 2 * rows
    f32, bf16 = jnp.float32, jnp.bfloat16

    def device(z_, x_, c_):
        return (z_ * 4 + x_ * 2 + c_, y)

    x_peer, sibling = device(z, 1 - x, core), device(z, x, 1 - core)
    y_peer = (node, 1 - y)
    z_peers = [None] + [device(flipped(z, k), x, core) for k in range(1, planes)]

    def block(x_, c_, size=rows):
        return pl.ds(pl.multiple_of((x_ * 2 + c_) * rows, rows), size)

    mine, here = block(x, core), block(y, 0, half)
    theirs = block(1 - y, 0, half)

    loads = [
        pltpu.make_async_copy(src.at[0], dst, w_sem.at[i])
        for i, (src, dst) in enumerate(((wg_hbm, wg), (wu_hbm, wu), (wd_hbm, wd)))
    ]
    for load in loads:
        load.start()

    barrier = pltpu.get_barrier_semaphore()
    peers = [x_peer, sibling, y_peer] + z_peers[1:]
    for peer in peers:
        pl.semaphore_signal(barrier, inc=1, device_id=peer, device_id_type=MESH)

    gath[0, mine, :feat] = tokens[...]
    gath[0, mine, feat : 2 * feat] = grad_out[...]
    lane = lax.broadcasted_iota(jnp.int32, (rows, LANES), 1)
    expert_lane = lax.rem(lane, experts)
    weight = jnp.zeros((rows, LANES), f32)
    for j in range(ids.shape[1]):
        weight = weight + jnp.where(expert_lane == ids[:, j : j + 1], gates[:, j : j + 1], 0.0)
    top = weight.astype(bf16).astype(f32)
    middle = (weight - top).astype(bf16).astype(f32)
    low = weight - top - middle
    packed = jnp.where(
        lane < experts, top, jnp.where(lane < 2 * experts, middle, jnp.where(lane < 3 * experts, low, 0.0))
    )
    gath[0, mine, 2 * feat :] = packed.astype(bf16)

    pl.semaphore_wait(barrier, len(peers))

    copies = {}

    def send(kind, k, src, dst, peer):
        copies[kind, k] = pltpu.make_async_remote_copy(
            src_ref=src, dst_ref=dst, send_sem=send_sem.at[k, kind], recv_sem=recv_sem.at[k, kind],
            device_id=peer, device_id_type=MESH,
        )
        copies[kind, k].start()

    def arrived(kind, k):
        copies[kind, k].wait_recv()

    def forward(kind, k, where, peer):
        send(kind, k, gath.at[k, where], gath.at[k, where], peer)

    def gather_column(k):
        if k:
            arrived(AG_Z, k)
        forward(AG_X, k, mine, x_peer)
        if k == 0:
            for far in range(1, planes):
                send(AG_Z, far, gath.at[0, mine], gath.at[far, mine], z_peers[far])
        forward(AG_A, k, mine, sibling)

    def gather_plane(k):
        arrived(AG_X, k)
        forward(AG_B, k, block(1 - x, core), sibling)

    def first_products(k):
        arrived(AG_A, k)
        arrived(AG_B, k)
        for m in range(3):
            if k == 0:
                loads[m].wait()

            def column_tile(j, carry, m=m):
                at = pl.ds(pl.multiple_of(j * TILE, TILE), TILE)
                if m < 2:
                    value = jnp.dot(gath[k, :, :feat], (wg, wu)[m][:, at], preferred_element_type=f32)
                else:
                    value = lax.dot_general(
                        gath[k, :, feat : 2 * feat], wd[at, :], NT, preferred_element_type=f32
                    )
                part[k, m, :, at] = value
                return carry

            lax.fori_loop(0, hidden // TILE, column_tile, 0)
            sum_send[k, m] = part[k, m, theirs, :].astype(bf16)
            send(SUM_Y + m, k, sum_send.at[k, m], sum_recv.at[k, m], y_peer)

    def hidden_grads(k):
        for m in range(3):
            arrived(SUM_Y + m, k)
        total = jnp.zeros((half, 1), f32)
        for j in range(hidden // TILE):
            at = pl.ds(j * TILE, TILE)
            gate, up, back = (
                part[k, m, here, at] + sum_recv[k, m, :, at].astype(f32) for m in range(3)
            )
            sig = jax.nn.sigmoid(gate)
            act = gate * sig
            back_act = back * act
            total = total + jnp.sum(back_act * up, axis=1, keepdims=True)
            grads[k, here, j * TILE : (j + 1) * TILE] = (
                back * up * sig * (1.0 + gate * (1.0 - sig))
            ).astype(bf16)
            grads[k, here, hidden + j * TILE : hidden + (j + 1) * TILE] = back_act.astype(bf16)
        lanes = lax.broadcasted_iota(jnp.int32, (half, LANES), 1)
        grads[k, here, 2 * hidden :] = jnp.where(lanes == node, total, 0.0).astype(bf16)
        send(GRAD_Y, k, grads.at[k, here], grads.at[k, here], y_peer)

    def second_products(k):
        arrived(GRAD_Y, k)
        lanes = lax.broadcasted_iota(jnp.int32, (2 * half, LANES), 1)
        chosen = (lax.rem(lanes, experts) == node) & (lanes < 3 * experts)
        scale = jnp.sum(
            jnp.where(chosen, gath[k, :, 2 * feat :].astype(f32), 0.0), axis=1, keepdims=True
        )

        def feature_tile(j, carry):
            at = pl.ds(pl.multiple_of(j * TILE, TILE), TILE)
            value = lax.dot_general(grads[k, :, :hidden], wg[at, :], NT, preferred_element_type=f32)
            value = value + lax.dot_general(
                grads[k, :, hidden : 2 * hidden], wu[at, :], NT, preferred_element_type=f32
            )
            pair[k, :, at] = value * scale
            return carry

        lax.fori_loop(0, feat // TILE, feature_tile, 0)
        pair[k, :, feat:] = grads[k, :, 2 * hidden :].astype(f32)
        for x_ in range(2):
            rc_send[k, x_] = pair[k, block(x_, 1 - core), :].astype(bf16)
        send(RS_C, k, rc_send.at[k], rc_recv.at[k], sibling)

    def chip_sum(k, x_):
        return pair[k, block(x_, core), :] + rc_recv[k, x_].astype(f32)

    def reduce_chip(k):
        arrived(RS_C, k)
        rx_send[k] = chip_sum(k, 1 - x).astype(bf16)
        send(RS_X, k, rx_send.at[k], rx_recv.at[k], x_peer)

    def reduce_plane(k):
        arrived(RS_X, k)
        value = chip_sum(k, x) + rx_recv[k].astype(f32)
        if k == 0:
            pair[0, mine, :] = value
        else:
            rz_send[k] = value.astype(bf16)
            send(RS_Z, k, rz_send.at[k], rz_recv.at[k], z_peers[k])

    stages = (
        (gather_column, 0), (gather_plane, 1), (first_products, 1), (reduce_chip, 4),
        (hidden_grads, 2), (second_products, 3), (reduce_plane, 5),
    )
    for turn in range(planes + 5):
        for stage, lag in stages:
            if 0 <= turn - lag < planes:
                stage(turn - lag)

    total = pair[0, mine, :]
    for k in range(1, planes):
        arrived(RS_Z, k)
        total = total + rz_recv[k].astype(f32)
    out[...] = total[:, :feat].astype(bf16)
    found = total[:, feat:]
    result = jnp.zeros(ids.shape, f32)
    slot = lax.broadcasted_iota(jnp.int32, ids.shape, 1)
    for j in range(ids.shape[1]):
        value = jnp.sum(jnp.where(lane == ids[:, j : j + 1], found, 0.0), axis=1, keepdims=True)
        result = result + jnp.where(slot == j, value, 0.0)
    out_gates[...] = result.astype(bf16)
    for copy in copies.values():
        copy.wait_send()


def dense_on_device(tokens, grad_out, gates, expert_ids, w_gate, w_up, w_down):
    planes = lax.axis_size("node") // 4
    rows, feat = tokens.shape
    hidden = w_gate.shape[2]
    bf16, f32 = jnp.bfloat16, jnp.float32
    wide = feat + LANES
    vmem, hbm = pl.BlockSpec(memory_space=pltpu.VMEM), pl.BlockSpec(memory_space=pl.ANY)
    return pl.pallas_call(
        functools.partial(dense_kernel, planes),
        out_shape=(
            jax.ShapeDtypeStruct((rows, feat), bf16),
            jax.ShapeDtypeStruct(expert_ids.shape, bf16),
        ),
        in_specs=[vmem] * 4 + [hbm] * 3,
        out_specs=(vmem, vmem),
        scratch_shapes=[
            pltpu.VMEM((feat, hidden), bf16),
            pltpu.VMEM((feat, hidden), bf16),
            pltpu.VMEM((hidden, feat), bf16),
            pltpu.VMEM((planes, 4 * rows, 2 * feat + LANES), bf16),
            pltpu.VMEM((planes, 3, 4 * rows, hidden), f32),
            pltpu.VMEM((planes, 3, 2 * rows, hidden), bf16),
            pltpu.VMEM((planes, 3, 2 * rows, hidden), bf16),
            pltpu.VMEM((planes, 4 * rows, 2 * hidden + LANES), bf16),
            pltpu.VMEM((planes, 4 * rows, wide), f32),
            pltpu.VMEM((planes, 2, rows, wide), bf16),
            pltpu.VMEM((planes, 2, rows, wide), bf16),
            pltpu.VMEM((planes, rows, wide), bf16),
            pltpu.VMEM((planes, rows, wide), bf16),
            pltpu.VMEM((planes, rows, wide), bf16),
            pltpu.VMEM((planes, rows, wide), bf16),
            pltpu.SemaphoreType.DMA((3,)),
            pltpu.SemaphoreType.DMA((planes, KINDS)),
            pltpu.SemaphoreType.DMA((planes, KINDS)),
        ],
        compiler_params=pltpu.CompilerParams(
            collective_id=0, has_side_effects=True, vmem_limit_bytes=56 * 1024 * 1024
        ),
    )(tokens, grad_out, gates, expert_ids, w_gate, w_up, w_down)


def local_grads(gate_pre, up_pre, back_pre, reduce_axis):
    sigmoid_gate = jax.nn.sigmoid(gate_pre)
    act = gate_pre * sigmoid_gate
    partial_gate = jnp.sum(act * up_pre * back_pre, axis=reduce_axis)
    grad_up = (back_pre * act).astype(jnp.bfloat16)
    grad_gate = (back_pre * up_pre * sigmoid_gate * (1.0 + gate_pre * (1.0 - sigmoid_gate))).astype(
        jnp.bfloat16
    )
    return (grad_gate, grad_up, partial_gate)


def on_device(tokens, grad_out, gates, expert_ids, w_gate, w_up, w_down):
    n_node = lax.axis_size("node")
    tok_rows, feature_cols = tokens.shape
    top_count = expert_ids.shape[1]
    capacity = min(tok_rows, max(2, 2 * tok_rows * top_count // n_node))
    planes = n_node // 4
    if capacity == tok_rows and n_node == 4 * planes and planes & (planes - 1) == 0 and 3 * n_node <= LANES:
        return dense_on_device(tokens, grad_out, gates, expert_ids, w_gate, w_up, w_down)
    flat_ids = expert_ids.reshape(-1)
    onehot = (flat_ids[:, None] == jnp.arange(n_node, dtype=jnp.int32)[None, :]).astype(jnp.int32)
    slot_rank = jnp.sum(onehot * (jnp.cumsum(onehot, axis=0) - 1), axis=1)
    target = flat_ids * capacity + slot_rank
    placed = (target[:, None] == jnp.arange(n_node * capacity, dtype=jnp.int32)[None, :]).astype(
        jnp.bfloat16
    )
    paired = jnp.repeat(jnp.concatenate([tokens, grad_out], axis=1), top_count, axis=0)
    outgoing = lax.dot_general(
        placed, paired, (((0,), (0,)), ((), ())), preferred_element_type=jnp.float32
    )
    outgoing = outgoing.astype(jnp.bfloat16).reshape(n_node, capacity, 2 * feature_cols)
    gate_cols = w_gate[0]
    up_cols = w_up[0]
    down_rows = w_down[0]
    incoming = lax.all_to_all(outgoing, "node", split_axis=0, concat_axis=0, tiled=True)
    sources = incoming.shape[0]
    slot_count = incoming.shape[1]
    row_count = sources * slot_count
    flat_in = incoming.reshape(row_count, 2 * feature_cols)
    x_rows = flat_in[:, :feature_cols]
    dy_rows = flat_in[:, feature_cols:]
    gate_pre = lax.dot_general(
        gate_cols, x_rows, (((0,), (1,)), ((), ())), preferred_element_type=jnp.float32
    )
    up_pre = lax.dot_general(
        up_cols, x_rows, (((0,), (1,)), ((), ())), preferred_element_type=jnp.float32
    )
    back_pre = lax.dot_general(
        down_rows, dy_rows, (((1,), (1,)), ((), ())), preferred_element_type=jnp.float32
    )
    summed = lax.psum_scatter(
        jnp.concatenate([gate_pre, up_pre, back_pre], axis=1),
        "local",
        scatter_dimension=0,
        tiled=True,
    )
    grad_gate, grad_up, partial_gate = local_grads(
        summed[:, :row_count], summed[:, row_count : 2 * row_count], summed[:, 2 * row_count :], 0
    )
    running = lax.dot_general(
        lax.all_gather(grad_gate, "local", axis=0, tiled=True),
        gate_cols,
        (((0,), (1,)), ((), ())),
        preferred_element_type=jnp.float32,
    )
    result = running + lax.dot_general(
        lax.all_gather(grad_up, "local", axis=0, tiled=True),
        up_cols,
        (((0,), (1,)), ((), ())),
        preferred_element_type=jnp.float32,
    )
    gate_total = lax.psum(partial_gate, "local").astype(jnp.bfloat16)
    sent_rows = result.astype(jnp.bfloat16).reshape(sources, slot_count, feature_cols)
    sent_gates = gate_total.reshape(sources, slot_count)
    back_rows = lax.all_to_all(sent_rows, "node", split_axis=0, concat_axis=0, tiled=True)
    back_gates = lax.all_to_all(sent_gates, "node", split_axis=0, concat_axis=0, tiled=True)
    picked = jnp.take(back_rows.reshape(n_node * capacity, feature_cols), target, axis=0)
    picked = picked.reshape(tok_rows, top_count, feature_cols).astype(jnp.float32)
    grad_tokens = jnp.sum(picked * gates[:, :, None], axis=1).astype(jnp.bfloat16)
    grad_gates = jnp.take(back_gates.reshape(-1), target, axis=0).reshape(tok_rows, top_count)
    return (grad_tokens, grad_gates)


def solution(mesh):
    in_specs = (
        P("node", "local"),
        P("node", "local"),
        P("node", None),
        P("node", None),
        P("node", "local", None),
        P("node", "local", None),
        P("node", None, "local"),
    )
    out_specs = (P("node", "local"), P("node", None))
    return jax.shard_map(
        on_device, mesh=mesh, in_specs=in_specs, out_specs=out_specs, check_vma=False
    )
```

```python
import functools

import jax
import jax.numpy as jnp
from jax import lax
from jax.experimental import pallas as pl
from jax.experimental.pallas import tpu as pltpu
from jax.sharding import PartitionSpec as P

MESH = pl.DeviceIdType.MESH
LANES = 128
TILE = 256
AG_Z, AG_X, AG_A, AG_B, SUM_Y, GRAD_Y, RS_C, RS_X, RS_Z, KINDS = 0, 1, 2, 3, 4, 7, 8, 9, 10, 11
NT = (((1,), (1,)), ((), ()))


def flipped(value, bits):
    place = 1
    while place <= bits:
        if bits & place:
            value = value + place * (1 - 2 * lax.rem(lax.div(value, place), 2))
        place *= 2
    return value


def dense_kernel(
    planes, tokens, grad_out, gates_t, ids_t, wg_hbm, wu_hbm, wd_hbm, out, out_gates,
    wg, wu, wd, gath, part, sum_send, sum_recv, grads, pair, rc_send, rc_recv,
    rx_send, rx_recv, rz_send, rz_recv, w_sem, send_sem, recv_sem,
):
    node, y = lax.axis_index("node"), lax.axis_index("local")
    core, x, z = lax.rem(node, 2), lax.rem(lax.div(node, 2), 2), lax.div(node, 4)
    rows, feat = tokens.shape
    hidden = wg.shape[1]
    experts = 4 * planes
    half = 2 * rows
    f32, bf16 = jnp.float32, jnp.bfloat16

    def device(z_, x_, c_):
        return (z_ * 4 + x_ * 2 + c_, y)

    x_peer, sibling = device(z, 1 - x, core), device(z, x, 1 - core)
    y_peer = (node, 1 - y)
    z_peers = [None] + [device(flipped(z, k), x, core) for k in range(1, planes)]

    def block(x_, c_, size=rows):
        return pl.ds(pl.multiple_of((x_ * 2 + c_) * rows, rows), size)

    mine = block(x, core)
    chunks = [(0, x * half, half, 0)]
    chunks += [(k, 0, 2 * half, 0) for k in range(1, planes)]
    chunks += [(0, (1 - x) * half, half, rows)]
    last = planes

    def part_rows(chunk, which):
        slot, base, size, place = chunks[chunk]
        return pl.ds(pl.multiple_of(base + which * (size // 2), rows), size // 2)

    def chunk_rows(chunk):
        slot, base, size, place = chunks[chunk]
        return pl.ds(base if isinstance(base, int) else pl.multiple_of(base, half), size)

    loads = [
        pltpu.make_async_copy(src.at[0], dst, w_sem.at[i])
        for i, (src, dst) in enumerate(((wg_hbm, wg), (wu_hbm, wu), (wd_hbm, wd)))
    ]
    for load in loads:
        load.start()

    barrier = pltpu.get_barrier_semaphore()
    peers = [x_peer, sibling, y_peer] + z_peers[1:]
    for peer in peers:
        pl.semaphore_signal(barrier, inc=1, device_id=peer, device_id_type=MESH)

    gath[0, mine, :feat] = tokens[...]
    gath[0, mine, feat : 2 * feat] = grad_out[...]
    lane = lax.broadcasted_iota(jnp.int32, (rows, LANES), 1)
    expert_lane = lax.rem(lane, experts)
    weight = jnp.zeros((rows, LANES), f32)
    top_count = ids_t.shape[0]
    diagonal = lax.broadcasted_iota(jnp.int32, (rows, rows), 0) == lax.broadcasted_iota(
        jnp.int32, (rows, rows), 1
    )

    def column(line):
        return jnp.sum(jnp.where(diagonal, line, 0.0), axis=1, keepdims=True)

    ids = [column(ids_t[j : j + 1, :].astype(f32)).astype(jnp.int32) for j in range(top_count)]
    for j in range(top_count):
        weight = weight + jnp.where(expert_lane == ids[j], column(gates_t[j : j + 1, :]), 0.0)
    top = weight.astype(bf16).astype(f32)
    middle = (weight - top).astype(bf16).astype(f32)
    low = weight - top - middle
    packed = jnp.where(
        lane < experts, top, jnp.where(lane < 2 * experts, middle, jnp.where(lane < 3 * experts, low, 0.0))
    )
    gath[0, mine, 2 * feat :] = packed.astype(bf16)

    pl.semaphore_wait(barrier, len(peers))

    copies = {}

    def send(kind, k, src, dst, peer):
        copies[kind, k] = pltpu.make_async_remote_copy(
            src_ref=src, dst_ref=dst, send_sem=send_sem.at[k, kind], recv_sem=recv_sem.at[k, kind],
            device_id=peer, device_id_type=MESH,
        )
        copies[kind, k].start()

    def arrived(kind, k):
        copies[kind, k].wait_recv()

    def forward(kind, k, where, peer):
        send(kind, k, gath.at[k, where], gath.at[k, where], peer)

    def gather_own():
        forward(AG_A, 0, mine, sibling)
        for k in range(1, planes):
            send(AG_Z, k, gath.at[0, mine], gath.at[k, mine], z_peers[k])

    def gather_column(k):
        if k:
            arrived(AG_Z, k)
        forward(AG_X, k, mine, x_peer)
        if k:
            forward(AG_A, k, mine, sibling)

    def gather_plane(k):
        arrived(AG_X, k)
        forward(AG_B, k, block(1 - x, core), sibling)

    def first_products(chunk, between=None):
        slot, base, size, place = chunks[chunk]
        where = chunk_rows(chunk)
        if chunk < last:
            arrived(AG_A, slot)
        if chunk > 0:
            arrived(AG_B, slot)
        for m in range(3):
            if chunk == 0:
                loads[m].wait()
            if m == 2 and between is not None:
                between()

            def column_tile(j, carry, m=m):
                at = pl.ds(pl.multiple_of(j * TILE, TILE), TILE)
                if m < 2:
                    value = jnp.dot(
                        gath[slot, where, :feat], (wg, wu)[m][:, at], preferred_element_type=f32
                    )
                else:
                    value = lax.dot_general(
                        gath[slot, where, feat : 2 * feat], wd[at, :], NT, preferred_element_type=f32
                    )
                part[slot, m, where, at] = value
                return carry

            lax.fori_loop(0, hidden // TILE, column_tile, 0)
            box = pl.ds(place, size // 2)
            sum_send[slot, m, box] = part[slot, m, part_rows(chunk, 1 - y), :].astype(bf16)
            send(SUM_Y + m, chunk, sum_send.at[slot, m, box], sum_recv.at[slot, m, box], y_peer)

    def hidden_grads(chunk):
        slot, base, size, place = chunks[chunk]
        here = part_rows(chunk, y)
        for m in range(3):
            arrived(SUM_Y + m, chunk)
        total = jnp.zeros((size // 2, 1), f32)
        for j in range(hidden // TILE):
            at = pl.ds(j * TILE, TILE)
            gate, up, back = (
                part[slot, m, here, at]
                + sum_recv[slot, m, place : place + size // 2, at].astype(f32)
                for m in range(3)
            )
            sig = jax.nn.sigmoid(gate)
            act = gate * sig
            back_act = back * act
            total = total + jnp.sum(back_act * up, axis=1, keepdims=True)
            grads[slot, here, j * TILE : (j + 1) * TILE] = (
                back * up * sig * (1.0 + gate * (1.0 - sig))
            ).astype(bf16)
            grads[slot, here, hidden + j * TILE : hidden + (j + 1) * TILE] = back_act.astype(bf16)
        lanes = lax.broadcasted_iota(jnp.int32, (size // 2, LANES), 1)
        grads[slot, here, 2 * hidden :] = jnp.where(lanes == node, total, 0.0).astype(bf16)
        send(GRAD_Y, chunk, grads.at[slot, here], grads.at[slot, here], y_peer)

    def second_products(chunk):
        slot, base, size, place = chunks[chunk]
        where = chunk_rows(chunk)
        arrived(GRAD_Y, chunk)
        lanes = lax.broadcasted_iota(jnp.int32, (size, LANES), 1)
        chosen = (lax.rem(lanes, experts) == node) & (lanes < 3 * experts)
        scale = jnp.sum(
            jnp.where(chosen, gath[slot, where, 2 * feat :].astype(f32), 0.0), axis=1, keepdims=True
        )

        def feature_tile(j, carry):
            at = pl.ds(pl.multiple_of(j * TILE, TILE), TILE)
            value = lax.dot_general(
                grads[slot, where, :hidden], wg[at, :], NT, preferred_element_type=f32
            )
            value = value + lax.dot_general(
                grads[slot, where, hidden : 2 * hidden], wu[at, :], NT, preferred_element_type=f32
            )
            pair[slot, where, at] = value * scale
            return carry

        lax.fori_loop(0, feat // TILE, feature_tile, 0)
        pair[slot, where, feat:] = grads[slot, where, 2 * hidden :].astype(f32)
        if chunk == 0:
            rc_send[0, 0] = pair[0, block(x, 1 - core), :].astype(bf16)
        elif chunk == last:
            rc_send[0, 1] = pair[0, block(1 - x, 1 - core), :].astype(bf16)
        else:
            for x_ in range(2):
                rc_send[slot, x_] = pair[slot, block(x_, 1 - core), :].astype(bf16)
        if chunk in (0, last):
            side = 0 if chunk == 0 else 1
            send(RS_C, chunk, rc_send.at[0, side], rc_recv.at[0, side], sibling)
        else:
            send(RS_C, chunk, rc_send.at[slot], rc_recv.at[slot], sibling)

    def reduce_chip(chunk):
        slot = chunks[chunk][0]
        arrived(RS_C, chunk)
        other = rc_recv[0, 1] if chunk == last else rc_recv[slot, 1 - x]
        rx_send[slot] = (pair[slot, block(1 - x, core), :] + other.astype(f32)).astype(bf16)
        send(RS_X, slot, rx_send.at[slot], rx_recv.at[slot], x_peer)

    def reduce_plane(k):
        arrived(RS_X, k)
        value = pair[k, mine, :] + rc_recv[k, x].astype(f32) + rx_recv[k].astype(f32)
        rz_send[k] = value.astype(bf16)
        send(RS_Z, k, rz_send.at[k], rz_recv.at[k], z_peers[k])

    gather_own()
    if planes > 1:
        first_products(0, lambda: gather_column(1))
    else:
        first_products(0)
    for k in range(1, planes):
        gather_plane(k)
        if k + 1 < planes:
            first_products(k, lambda: gather_column(k + 1))
        else:
            gather_column(0)
            first_products(k)
        hidden_grads(k - 1)
        if k >= 2:
            second_products(k - 2)
        if k >= 4:
            reduce_chip(k - 3)
        if k >= 5:
            reduce_plane(k - 4)
    if planes == 1:
        gather_column(0)
    gather_plane(0)
    first_products(last)
    hidden_grads(last - 1)
    if planes >= 2:
        second_products(last - 2)
    if planes >= 4:
        reduce_chip(last - 3)
    if planes >= 5:
        reduce_plane(last - 4)
    hidden_grads(last)
    if planes >= 3:
        reduce_chip(last - 2)
    if planes >= 4:
        reduce_plane(last - 3)
    second_products(last - 1)
    if planes >= 3:
        reduce_plane(last - 2)
    if planes >= 2:
        reduce_chip(last - 1)
    second_products(last)
    if planes >= 2:
        reduce_plane(last - 1)
    reduce_chip(last)

    arrived(RS_C, 0)
    total = pair[0, mine, :] + rc_recv[0, 0].astype(f32)
    for k in range(1, planes):
        arrived(RS_Z, k)
        total = total + rz_recv[k].astype(f32)
    arrived(RS_X, 0)
    total = total + rx_recv[0].astype(f32)
    out[...] = total[:, :feat].astype(bf16)
    found = total[:, feat:]
    for j in range(top_count):
        value = jnp.sum(jnp.where(lane == ids[j], found, 0.0), axis=1, keepdims=True)
        line = jnp.sum(jnp.where(diagonal, value, 0.0), axis=0, keepdims=True)
        out_gates[j : j + 1, :] = line.astype(bf16)
    for copy in copies.values():
        copy.wait_send()


def dense_on_device(tokens, grad_out, gates, expert_ids, w_gate, w_up, w_down):
    planes = lax.axis_size("node") // 4
    rows, feat = tokens.shape
    hidden = w_gate.shape[2]
    bf16, f32 = jnp.bfloat16, jnp.float32
    wide = feat + LANES
    vmem, hbm = pl.BlockSpec(memory_space=pltpu.VMEM), pl.BlockSpec(memory_space=pl.ANY)
    grad_tokens, grad_gates_t = pl.pallas_call(
        functools.partial(dense_kernel, planes),
        out_shape=(
            jax.ShapeDtypeStruct((rows, feat), bf16),
            jax.ShapeDtypeStruct(expert_ids.shape[::-1], bf16),
        ),
        in_specs=[vmem] * 4 + [hbm] * 3,
        out_specs=(vmem, vmem),
        scratch_shapes=[
            pltpu.VMEM((feat, hidden), bf16),
            pltpu.VMEM((feat, hidden), bf16),
            pltpu.VMEM((hidden, feat), bf16),
            pltpu.VMEM((planes, 4 * rows, 2 * feat + LANES), bf16),
            pltpu.VMEM((planes, 3, 4 * rows, hidden), f32),
            pltpu.VMEM((planes, 3, 2 * rows, hidden), bf16),
            pltpu.VMEM((planes, 3, 2 * rows, hidden), bf16),
            pltpu.VMEM((planes, 4 * rows, 2 * hidden + LANES), bf16),
            pltpu.VMEM((planes, 4 * rows, wide), f32),
            pltpu.VMEM((planes, 2, rows, wide), bf16),
            pltpu.VMEM((planes, 2, rows, wide), bf16),
            pltpu.VMEM((planes, rows, wide), bf16),
            pltpu.VMEM((planes, rows, wide), bf16),
            pltpu.VMEM((planes, rows, wide), bf16),
            pltpu.VMEM((planes, rows, wide), bf16),
            pltpu.SemaphoreType.DMA((3,)),
            pltpu.SemaphoreType.DMA((planes + 1, KINDS)),
            pltpu.SemaphoreType.DMA((planes + 1, KINDS)),
        ],
        compiler_params=pltpu.CompilerParams(
            collective_id=0, has_side_effects=True, vmem_limit_bytes=56 * 1024 * 1024
        ),
    )(tokens, grad_out, gates.T, expert_ids.T, w_gate, w_up, w_down)
    return grad_tokens, grad_gates_t.T


def local_grads(gate_pre, up_pre, back_pre, reduce_axis):
    sigmoid_gate = jax.nn.sigmoid(gate_pre)
    act = gate_pre * sigmoid_gate
    partial_gate = jnp.sum(act * up_pre * back_pre, axis=reduce_axis)
    grad_up = (back_pre * act).astype(jnp.bfloat16)
    grad_gate = (back_pre * up_pre * sigmoid_gate * (1.0 + gate_pre * (1.0 - sigmoid_gate))).astype(
        jnp.bfloat16
    )
    return (grad_gate, grad_up, partial_gate)


def on_device(tokens, grad_out, gates, expert_ids, w_gate, w_up, w_down):
    n_node = lax.axis_size("node")
    tok_rows, feature_cols = tokens.shape
    top_count = expert_ids.shape[1]
    capacity = min(tok_rows, max(2, 2 * tok_rows * top_count // n_node))
    planes = n_node // 4
    if capacity == tok_rows and n_node == 4 * planes and planes & (planes - 1) == 0 and 3 * n_node <= LANES:
        return dense_on_device(tokens, grad_out, gates, expert_ids, w_gate, w_up, w_down)
    flat_ids = expert_ids.reshape(-1)
    onehot = (flat_ids[:, None] == jnp.arange(n_node, dtype=jnp.int32)[None, :]).astype(jnp.int32)
    slot_rank = jnp.sum(onehot * (jnp.cumsum(onehot, axis=0) - 1), axis=1)
    target = flat_ids * capacity + slot_rank
    placed = (target[:, None] == jnp.arange(n_node * capacity, dtype=jnp.int32)[None, :]).astype(
        jnp.bfloat16
    )
    paired = jnp.repeat(jnp.concatenate([tokens, grad_out], axis=1), top_count, axis=0)
    outgoing = lax.dot_general(
        placed, paired, (((0,), (0,)), ((), ())), preferred_element_type=jnp.float32
    )
    outgoing = outgoing.astype(jnp.bfloat16).reshape(n_node, capacity, 2 * feature_cols)
    gate_cols = w_gate[0]
    up_cols = w_up[0]
    down_rows = w_down[0]
    incoming = lax.all_to_all(outgoing, "node", split_axis=0, concat_axis=0, tiled=True)
    sources = incoming.shape[0]
    slot_count = incoming.shape[1]
    row_count = sources * slot_count
    flat_in = incoming.reshape(row_count, 2 * feature_cols)
    x_rows = flat_in[:, :feature_cols]
    dy_rows = flat_in[:, feature_cols:]
    gate_pre = lax.dot_general(
        gate_cols, x_rows, (((0,), (1,)), ((), ())), preferred_element_type=jnp.float32
    )
    up_pre = lax.dot_general(
        up_cols, x_rows, (((0,), (1,)), ((), ())), preferred_element_type=jnp.float32
    )
    back_pre = lax.dot_general(
        down_rows, dy_rows, (((1,), (1,)), ((), ())), preferred_element_type=jnp.float32
    )
    summed = lax.psum_scatter(
        jnp.concatenate([gate_pre, up_pre, back_pre], axis=1),
        "local",
        scatter_dimension=0,
        tiled=True,
    )
    grad_gate, grad_up, partial_gate = local_grads(
        summed[:, :row_count], summed[:, row_count : 2 * row_count], summed[:, 2 * row_count :], 0
    )
    running = lax.dot_general(
        lax.all_gather(grad_gate, "local", axis=0, tiled=True),
        gate_cols,
        (((0,), (1,)), ((), ())),
        preferred_element_type=jnp.float32,
    )
    result = running + lax.dot_general(
        lax.all_gather(grad_up, "local", axis=0, tiled=True),
        up_cols,
        (((0,), (1,)), ((), ())),
        preferred_element_type=jnp.float32,
    )
    gate_total = lax.psum(partial_gate, "local").astype(jnp.bfloat16)
    sent_rows = result.astype(jnp.bfloat16).reshape(sources, slot_count, feature_cols)
    sent_gates = gate_total.reshape(sources, slot_count)
    back_rows = lax.all_to_all(sent_rows, "node", split_axis=0, concat_axis=0, tiled=True)
    back_gates = lax.all_to_all(sent_gates, "node", split_axis=0, concat_axis=0, tiled=True)
    picked = jnp.take(back_rows.reshape(n_node * capacity, feature_cols), target, axis=0)
    picked = picked.reshape(tok_rows, top_count, feature_cols).astype(jnp.float32)
    grad_tokens = jnp.sum(picked * gates[:, :, None], axis=1).astype(jnp.bfloat16)
    grad_gates = jnp.take(back_gates.reshape(-1), target, axis=0).reshape(tok_rows, top_count)
    return (grad_tokens, grad_gates)


def solution(mesh):
    in_specs = (
        P("node", "local"),
        P("node", "local"),
        P("node", None),
        P("node", None),
        P("node", "local", None),
        P("node", "local", None),
        P("node", None, "local"),
    )
    out_specs = (P("node", "local"), P("node", None))
    return jax.shard_map(
        on_device, mesh=mesh, in_specs=in_specs, out_specs=out_specs, check_vma=False
    )
```

```python
import functools

import jax
import jax.numpy as jnp
from jax import lax
from jax.experimental import pallas as pl
from jax.experimental.pallas import tpu as pltpu
from jax.sharding import PartitionSpec as P

MESH = pl.DeviceIdType.MESH
LANES = 128
TILE = 256
NT = (((1,), (1,)), ((), ()))


def flipped(value, bits):
    place = 1
    while place <= bits:
        if bits & place:
            value = value + place * (1 - 2 * lax.rem(lax.div(value, place), 2))
        place *= 2
    return value


def dense_kernel(
    planes, tokens, grad_out, gates_t, ids_t, wg_hbm, wu_hbm, wd_hbm, out, out_gates,
    wg, wu, wd, gath, part, sum_send, sum_recv, grads, gate_sums, pair, rc_send, rc_recv,
    rx_send, rx_recv, rz_send, rz_recv, w_sem, send_sem, recv_sem,
):
    node, y = lax.axis_index("node"), lax.axis_index("local")
    core, x, z = lax.rem(node, 2), lax.rem(lax.div(node, 2), 2), lax.div(node, 4)
    rows, feat = tokens.shape
    hidden = wg.shape[1]
    experts = 4 * planes
    plane = 4 * rows
    tiles = hidden // TILE
    f32, bf16 = jnp.float32, jnp.bfloat16
    halves = ((0, feat // 2), (feat // 2, feat + LANES))

    def device(z_, x_, c_):
        return (z_ * 4 + x_ * 2 + c_, y)

    x_peer, sibling = device(z, 1 - x, core), device(z, x, 1 - core)
    y_peer = (node, 1 - y)
    z_peers = [None] + [device(flipped(z, k), x, core) for k in range(1, planes)]

    def block(k, x_, c_):
        return pl.ds(pl.multiple_of(k * plane + (x_ * 2 + c_) * rows, rows), rows)

    def plane_rows(k):
        return pl.ds(pl.multiple_of(k * plane, plane), plane)

    mine = block(0, x, core)

    loads = [
        pltpu.make_async_copy(src.at[0], dst, w_sem.at[i])
        for i, (src, dst) in enumerate(((wg_hbm, wg), (wu_hbm, wu), (wd_hbm, wd)))
    ]
    for load in loads:
        load.start()

    barrier = pltpu.get_barrier_semaphore()
    peers = [x_peer, sibling, y_peer] + z_peers[1:]
    for peer in peers:
        pl.semaphore_signal(barrier, inc=1, device_id=peer, device_id_type=MESH)

    gath[mine, :feat] = tokens[...]
    gath[mine, feat : 2 * feat] = grad_out[...]
    lane = lax.broadcasted_iota(jnp.int32, (rows, LANES), 1)
    expert_lane = lax.rem(lane, experts)
    weight = jnp.zeros((rows, LANES), f32)
    top_count = ids_t.shape[0]
    diagonal = lax.broadcasted_iota(jnp.int32, (rows, rows), 0) == lax.broadcasted_iota(
        jnp.int32, (rows, rows), 1
    )

    def column(line):
        return jnp.sum(jnp.where(diagonal, line, 0.0), axis=1, keepdims=True)

    ids = [column(ids_t[j : j + 1, :].astype(f32)).astype(jnp.int32) for j in range(top_count)]
    for j in range(top_count):
        weight = weight + jnp.where(expert_lane == ids[j], column(gates_t[j : j + 1, :]), 0.0)
    top = weight.astype(bf16).astype(f32)
    middle = (weight - top).astype(bf16).astype(f32)
    low = weight - top - middle
    packed = jnp.where(
        lane < experts, top, jnp.where(lane < 2 * experts, middle, jnp.where(lane < 3 * experts, low, 0.0))
    )
    gath[mine, 2 * feat :] = packed.astype(bf16)

    pl.semaphore_wait(barrier, len(peers))

    copies = {}

    def send(name, src, dst, peer):
        i = len(copies)
        copies[name] = pltpu.make_async_remote_copy(
            src_ref=src, dst_ref=dst, send_sem=send_sem.at[i], recv_sem=recv_sem.at[i],
            device_id=peer, device_id_type=MESH,
        )
        copies[name].start()

    def arrived(*name):
        copies[name].wait_recv()

    def forward(name, where, peer):
        send(name, gath.at[where], gath.at[where], peer)

    def gather_own():
        forward(("x", 0), mine, x_peer)
        for k in range(1, planes):
            send(("z", k), gath.at[mine], gath.at[block(k, x, core)], z_peers[k])
        forward(("a", 0), mine, sibling)

    def gather_column(k):
        arrived("z", k)
        forward(("x", k), block(k, x, core), x_peer)
        forward(("a", k), block(k, x, core), sibling)

    def gather_plane(k):
        arrived("x", k)
        forward(("b", k), block(k, 1 - x, core), sibling)

    def first_products(ch, j):
        where, at = pl.ds(ch * 2 * plane, 2 * plane), pl.ds(j * TILE, TILE)
        if j == 0:
            for k in (2 * ch, 2 * ch + 1):
                arrived("a", k)
                arrived("b", k)
        for m in range(3):
            if ch == 0 and j == 0:
                loads[m].wait()
            if m < 2:
                value = jnp.dot(gath[where, :feat], (wg, wu)[m][:, at], preferred_element_type=f32)
            else:
                value = lax.dot_general(
                    gath[where, feat : 2 * feat], wd[at, :], NT, preferred_element_type=f32
                )
            part[m, where, at] = value
            sum_send[ch, j, m] = part[m, plane_rows(2 * ch + 1 - y), at].astype(bf16)
        send(("sum", ch, j), sum_send.at[ch, j], sum_recv.at[ch, j], y_peer)

    gate_totals = {}

    def hidden_grads(ch, j):
        here, at = plane_rows(2 * ch + y), pl.ds(j * TILE, TILE)
        arrived("sum", ch, j)
        gate, up, back = (part[m, here, at] + sum_recv[ch, j, m].astype(f32) for m in range(3))
        sig = jax.nn.sigmoid(gate)
        act = gate * sig
        back_act = back * act
        total = jnp.sum(back_act * up, axis=1, keepdims=True)
        gate_totals[ch] = gate_totals[ch] + total if j else total
        grads[j, here, :TILE] = (back * up * sig * (1.0 + gate * (1.0 - sig))).astype(bf16)
        grads[j, here, TILE:] = back_act.astype(bf16)
        send(("grad", ch, j), grads.at[j, here], grads.at[j, here], y_peer)
        if j == tiles - 1:
            lanes = lax.broadcasted_iota(jnp.int32, (plane, LANES), 1)
            gate_sums[here] = jnp.where(lanes == node, gate_totals[ch], 0.0).astype(bf16)
            send(("gates", ch), gate_sums.at[here], gate_sums.at[here], y_peer)

    def second_products(ch, h):
        where = pl.ds(ch * 2 * plane, 2 * plane)
        if h == 0:
            for j in range(tiles):
                arrived("grad", ch, j)
        lanes = lax.broadcasted_iota(jnp.int32, (2 * plane, LANES), 1)
        chosen = (lax.rem(lanes, experts) == node) & (lanes < 3 * experts)
        scale = jnp.sum(
            jnp.where(chosen, gath[where, 2 * feat :].astype(f32), 0.0), axis=1, keepdims=True
        )

        def feature_tile(i, carry):
            at = pl.ds(pl.multiple_of(i * TILE, TILE), TILE)
            value = jnp.zeros((2 * plane, TILE), f32)
            for j in range(tiles):
                for m in range(2):
                    value = value + lax.dot_general(
                        grads[j, where, m * TILE : (m + 1) * TILE],
                        (wg, wu)[m][at, j * TILE : (j + 1) * TILE],
                        NT,
                        preferred_element_type=f32,
                    )
            pair[where, at] = value * scale
            return carry

        lax.fori_loop(h * feat // 2 // TILE, (h + 1) * feat // 2 // TILE, feature_tile, 0)
        if h == 1:
            arrived("gates", ch)
            pair[where, feat:] = gate_sums[where].astype(f32)
        lo, hi = halves[h]
        for k in (2 * ch, 2 * ch + 1):
            for x_ in range(2):
                rc_send[k, x_, :, lo:hi] = pair[block(k, x_, 1 - core), lo:hi].astype(bf16)
        box = (pl.ds(2 * ch, 2), slice(None), slice(None), pl.ds(lo, hi - lo))
        send(("core", ch, h), rc_send.at[box], rc_recv.at[box], sibling)

    def reduce_chip(ch, h):
        lo, hi = halves[h]
        arrived("core", ch, h)
        for k in (2 * ch, 2 * ch + 1):
            value = pair[block(k, 1 - x, core), lo:hi] + rc_recv[k, 1 - x, :, lo:hi].astype(f32)
            rx_send[k, :, lo:hi] = value.astype(bf16)
        box = (pl.ds(2 * ch, 2), slice(None), pl.ds(lo, hi - lo))
        send(("across", ch, h), rx_send.at[box], rx_recv.at[box], x_peer)

    def reduce_plane(ch, h):
        lo, hi = halves[h]
        arrived("across", ch, h)
        for k in (2 * ch, 2 * ch + 1):
            value = pair[block(k, x, core), lo:hi] + rc_recv[k, x, :, lo:hi].astype(f32)
            value = value + rx_recv[k, :, lo:hi].astype(f32)
            if k == 0:
                pair[mine, lo:hi] = value
            else:
                rz_send[k, :, lo:hi] = value.astype(bf16)
                box = (k, slice(None), pl.ds(lo, hi - lo))
                send(("home", k, h), rz_send.at[box], rz_recv.at[box], z_peers[k])

    count = planes // 2
    gather_own()
    gather_column(1)
    gather_plane(0)
    gather_plane(1)
    for ch in range(count):
        ahead = []
        if ch + 1 < count:
            k = 2 * ch + 2
            ahead = [(gather_column, k), (gather_column, k + 1), (gather_plane, k), (gather_plane, k + 1)]
        for j in range(tiles):
            first_products(ch, j)
            if j < len(ahead):
                ahead[j][0](ahead[j][1])
            if ch:
                hidden_grads(ch - 1, j)
        for stage, k in ahead[tiles:]:
            stage(k)
    for j in range(tiles):
        hidden_grads(count - 1, j)
    for ch in range(count + 1):
        for h in range(2):
            if ch < count:
                second_products(ch, h)
            if ch:
                reduce_chip(ch - 1, h)
        if ch:
            for h in range(2):
                reduce_plane(ch - 1, h)

    found = None
    for h, (lo, hi) in enumerate(halves):
        total = pair[mine, lo:hi]
        for k in range(1, planes):
            arrived("home", k, h)
            total = total + rz_recv[k, :, lo:hi].astype(f32)
        out[:, lo : min(hi, feat)] = total[:, : min(hi, feat) - lo].astype(bf16)
        found = total[:, hi - lo - LANES :]
    for j in range(top_count):
        value = jnp.sum(jnp.where(lane == ids[j], found, 0.0), axis=1, keepdims=True)
        line = jnp.sum(jnp.where(diagonal, value, 0.0), axis=0, keepdims=True)
        out_gates[j : j + 1, :] = line.astype(bf16)
    for copy in copies.values():
        copy.wait_send()


def dense_on_device(tokens, grad_out, gates, expert_ids, w_gate, w_up, w_down):
    planes = lax.axis_size("node") // 4
    rows, feat = tokens.shape
    hidden = w_gate.shape[2]
    bf16, f32 = jnp.bfloat16, jnp.float32
    wide, tiles = feat + LANES, hidden // TILE
    vmem, hbm = pl.BlockSpec(memory_space=pltpu.VMEM), pl.BlockSpec(memory_space=pl.ANY)
    grad_tokens, grad_gates_t = pl.pallas_call(
        functools.partial(dense_kernel, planes),
        out_shape=(
            jax.ShapeDtypeStruct((rows, feat), bf16),
            jax.ShapeDtypeStruct(expert_ids.shape[::-1], bf16),
        ),
        in_specs=[vmem] * 4 + [hbm] * 3,
        out_specs=(vmem, vmem),
        scratch_shapes=[
            pltpu.VMEM((feat, hidden), bf16),
            pltpu.VMEM((feat, hidden), bf16),
            pltpu.VMEM((hidden, feat), bf16),
            pltpu.VMEM((planes * 4 * rows, 2 * feat + LANES), bf16),
            pltpu.VMEM((3, planes * 4 * rows, hidden), f32),
            pltpu.VMEM((planes // 2, tiles, 3, 4 * rows, TILE), bf16),
            pltpu.VMEM((planes // 2, tiles, 3, 4 * rows, TILE), bf16),
            pltpu.VMEM((tiles, planes * 4 * rows, 2 * TILE), bf16),
            pltpu.VMEM((planes * 4 * rows, LANES), bf16),
            pltpu.VMEM((planes * 4 * rows, wide), f32),
            pltpu.VMEM((planes, 2, rows, wide), bf16),
            pltpu.VMEM((planes, 2, rows, wide), bf16),
            pltpu.VMEM((planes, rows, wide), bf16),
            pltpu.VMEM((planes, rows, wide), bf16),
            pltpu.VMEM((planes, rows, wide), bf16),
            pltpu.VMEM((planes, rows, wide), bf16),
            pltpu.SemaphoreType.DMA((3,)),
            pltpu.SemaphoreType.DMA((planes * (8 + tiles),)),
            pltpu.SemaphoreType.DMA((planes * (8 + tiles),)),
        ],
        compiler_params=pltpu.CompilerParams(
            collective_id=0, has_side_effects=True, vmem_limit_bytes=56 * 1024 * 1024
        ),
    )(tokens, grad_out, gates.T, expert_ids.T, w_gate, w_up, w_down)
    return grad_tokens, grad_gates_t.T


def local_grads(gate_pre, up_pre, back_pre, reduce_axis):
    sigmoid_gate = jax.nn.sigmoid(gate_pre)
    act = gate_pre * sigmoid_gate
    partial_gate = jnp.sum(act * up_pre * back_pre, axis=reduce_axis)
    grad_up = (back_pre * act).astype(jnp.bfloat16)
    grad_gate = (back_pre * up_pre * sigmoid_gate * (1.0 + gate_pre * (1.0 - sigmoid_gate))).astype(
        jnp.bfloat16
    )
    return (grad_gate, grad_up, partial_gate)


def on_device(tokens, grad_out, gates, expert_ids, w_gate, w_up, w_down):
    n_node = lax.axis_size("node")
    tok_rows, feature_cols = tokens.shape
    top_count = expert_ids.shape[1]
    capacity = min(tok_rows, max(2, 2 * tok_rows * top_count // n_node))
    planes = n_node // 4
    if capacity == tok_rows and n_node == 4 * planes and planes > 1 and planes & (planes - 1) == 0 and 3 * n_node <= LANES:
        return dense_on_device(tokens, grad_out, gates, expert_ids, w_gate, w_up, w_down)
    flat_ids = expert_ids.reshape(-1)
    onehot = (flat_ids[:, None] == jnp.arange(n_node, dtype=jnp.int32)[None, :]).astype(jnp.int32)
    slot_rank = jnp.sum(onehot * (jnp.cumsum(onehot, axis=0) - 1), axis=1)
    target = flat_ids * capacity + slot_rank
    placed = (target[:, None] == jnp.arange(n_node * capacity, dtype=jnp.int32)[None, :]).astype(
        jnp.bfloat16
    )
    paired = jnp.repeat(jnp.concatenate([tokens, grad_out], axis=1), top_count, axis=0)
    outgoing = lax.dot_general(
        placed, paired, (((0,), (0,)), ((), ())), preferred_element_type=jnp.float32
    )
    outgoing = outgoing.astype(jnp.bfloat16).reshape(n_node, capacity, 2 * feature_cols)
    gate_cols = w_gate[0]
    up_cols = w_up[0]
    down_rows = w_down[0]
    incoming = lax.all_to_all(outgoing, "node", split_axis=0, concat_axis=0, tiled=True)
    sources = incoming.shape[0]
    slot_count = incoming.shape[1]
    row_count = sources * slot_count
    flat_in = incoming.reshape(row_count, 2 * feature_cols)
    x_rows = flat_in[:, :feature_cols]
    dy_rows = flat_in[:, feature_cols:]
    gate_pre = lax.dot_general(
        gate_cols, x_rows, (((0,), (1,)), ((), ())), preferred_element_type=jnp.float32
    )
    up_pre = lax.dot_general(
        up_cols, x_rows, (((0,), (1,)), ((), ())), preferred_element_type=jnp.float32
    )
    back_pre = lax.dot_general(
        down_rows, dy_rows, (((1,), (1,)), ((), ())), preferred_element_type=jnp.float32
    )
    summed = lax.psum_scatter(
        jnp.concatenate([gate_pre, up_pre, back_pre], axis=1),
        "local",
        scatter_dimension=0,
        tiled=True,
    )
    grad_gate, grad_up, partial_gate = local_grads(
        summed[:, :row_count], summed[:, row_count : 2 * row_count], summed[:, 2 * row_count :], 0
    )
    running = lax.dot_general(
        lax.all_gather(grad_gate, "local", axis=0, tiled=True),
        gate_cols,
        (((0,), (1,)), ((), ())),
        preferred_element_type=jnp.float32,
    )
    result = running + lax.dot_general(
        lax.all_gather(grad_up, "local", axis=0, tiled=True),
        up_cols,
        (((0,), (1,)), ((), ())),
        preferred_element_type=jnp.float32,
    )
    gate_total = lax.psum(partial_gate, "local").astype(jnp.bfloat16)
    sent_rows = result.astype(jnp.bfloat16).reshape(sources, slot_count, feature_cols)
    sent_gates = gate_total.reshape(sources, slot_count)
    back_rows = lax.all_to_all(sent_rows, "node", split_axis=0, concat_axis=0, tiled=True)
    back_gates = lax.all_to_all(sent_gates, "node", split_axis=0, concat_axis=0, tiled=True)
    picked = jnp.take(back_rows.reshape(n_node * capacity, feature_cols), target, axis=0)
    picked = picked.reshape(tok_rows, top_count, feature_cols).astype(jnp.float32)
    grad_tokens = jnp.sum(picked * gates[:, :, None], axis=1).astype(jnp.bfloat16)
    grad_gates = jnp.take(back_gates.reshape(-1), target, axis=0).reshape(tok_rows, top_count)
    return (grad_tokens, grad_gates)


def solution(mesh):
    in_specs = (
        P("node", "local"),
        P("node", "local"),
        P("node", None),
        P("node", None),
        P("node", "local", None),
        P("node", "local", None),
        P("node", None, "local"),
    )
    out_specs = (P("node", "local"), P("node", None))
    return jax.shard_map(
        on_device, mesh=mesh, in_specs=in_specs, out_specs=out_specs, check_vma=False
    )
```

```python
import functools

import jax
import jax.numpy as jnp
from jax import lax
from jax.experimental import pallas as pl
from jax.experimental.pallas import tpu as pltpu
from jax.sharding import PartitionSpec as P

MESH = pl.DeviceIdType.MESH
LANES = 128
TILE = 256
NT = (((1,), (1,)), ((), ()))


def flipped(value, bits):
    place = 1
    while place <= bits:
        if bits & place:
            value = value + place * (1 - 2 * lax.rem(lax.div(value, place), 2))
        place *= 2
    return value


def dense_kernel(
    planes, tokens, grad_out, gates_t, ids_t, wg_hbm, wu_hbm, wd_hbm, out, out_gates,
    wg, wu, wd, gath, part, sum_send, sum_recv, grads, gate_sums, pair, rc_send, rc_recv,
    rx_send, rx_recv, rz_send, rz_recv, w_sem, send_sem, recv_sem,
):
    node, y = lax.axis_index("node"), lax.axis_index("local")
    core, x, z = lax.rem(node, 2), lax.rem(lax.div(node, 2), 2), lax.div(node, 4)
    rows, feat = tokens.shape
    hidden = wg.shape[1]
    experts = 4 * planes
    plane = 4 * rows
    tiles = hidden // TILE
    f32, bf16 = jnp.float32, jnp.bfloat16
    halves = ((0, feat // 2), (feat // 2, feat + LANES))

    def device(z_, x_, c_):
        return (z_ * 4 + x_ * 2 + c_, y)

    x_peer, sibling = device(z, 1 - x, core), device(z, x, 1 - core)
    y_peer = (node, 1 - y)
    z_peers = [None] + [device(flipped(z, k), x, core) for k in range(1, planes)]

    def block(k, x_, c_):
        return pl.ds(pl.multiple_of(k * plane + (x_ * 2 + c_) * rows, rows), rows)

    mine = block(0, x, core)
    chunks = [(0, 1)] + ([(1, 1)] if planes > 2 else []) + [(planes // 2, planes - planes // 2)]
    last = len(chunks) - 1

    def chunk_planes(ch):
        return range(chunks[ch][0], chunks[ch][0] + chunks[ch][1])

    def chunk_rows(ch):
        return pl.ds(chunks[ch][0] * plane, chunks[ch][1] * plane)

    def part_rows(ch, which):
        size = chunks[ch][1] * plane // 2
        return pl.ds(pl.multiple_of(chunks[ch][0] * plane + which * size, 2 * rows), size)

    def part_box(ch):
        return pl.ds(chunks[ch][0] * plane // 2, chunks[ch][1] * plane // 2)

    loads = [
        pltpu.make_async_copy(src.at[0], dst, w_sem.at[i])
        for i, (src, dst) in enumerate(((wg_hbm, wg), (wu_hbm, wu), (wd_hbm, wd)))
    ]
    for load in loads:
        load.start()

    barrier = pltpu.get_barrier_semaphore()
    peers = [x_peer, sibling, y_peer] + z_peers[1:]
    for peer in peers:
        pl.semaphore_signal(barrier, inc=1, device_id=peer, device_id_type=MESH)

    gath[mine, :feat] = tokens[...]
    gath[mine, feat : 2 * feat] = grad_out[...]
    lane = lax.broadcasted_iota(jnp.int32, (rows, LANES), 1)
    expert_lane = lax.rem(lane, experts)
    weight = jnp.zeros((rows, LANES), f32)
    top_count = ids_t.shape[0]
    diagonal = lax.broadcasted_iota(jnp.int32, (rows, rows), 0) == lax.broadcasted_iota(
        jnp.int32, (rows, rows), 1
    )

    def column(line):
        return jnp.sum(jnp.where(diagonal, line, 0.0), axis=1, keepdims=True)

    ids = [column(ids_t[j : j + 1, :].astype(f32)).astype(jnp.int32) for j in range(top_count)]
    for j in range(top_count):
        weight = weight + jnp.where(expert_lane == ids[j], column(gates_t[j : j + 1, :]), 0.0)
    top = weight.astype(bf16).astype(f32)
    middle = (weight - top).astype(bf16).astype(f32)
    low = weight - top - middle
    packed = jnp.where(
        lane < experts, top, jnp.where(lane < 2 * experts, middle, jnp.where(lane < 3 * experts, low, 0.0))
    )
    gath[mine, 2 * feat :] = packed.astype(bf16)

    pl.semaphore_wait(barrier, len(peers))

    copies = {}

    def send(name, src, dst, peer):
        i = len(copies)
        copies[name] = pltpu.make_async_remote_copy(
            src_ref=src, dst_ref=dst, send_sem=send_sem.at[i], recv_sem=recv_sem.at[i],
            device_id=peer, device_id_type=MESH,
        )
        copies[name].start()

    def arrived(*name):
        copies[name].wait_recv()

    def forward(name, where, peer):
        send(name, gath.at[where], gath.at[where], peer)

    def send_far(k):
        send(("z", k), gath.at[mine], gath.at[block(k, x, core)], z_peers[k])

    def gather_own():
        forward(("x", 0), mine, x_peer)
        send_far(1)
        forward(("a", 0), mine, sibling)

    def gather_column(k):
        arrived("z", k)
        forward(("x", k), block(k, x, core), x_peer)
        forward(("a", k), block(k, x, core), sibling)

    def gather_plane(k):
        arrived("x", k)
        forward(("b", k), block(k, 1 - x, core), sibling)

    def first_products(ch, j):
        where, at, box = chunk_rows(ch), pl.ds(j * TILE, TILE), part_box(ch)
        if j == 0:
            for k in chunk_planes(ch):
                arrived("a", k)
                arrived("b", k)
        for m in range(3):
            if ch == 0 and j == 0:
                loads[m].wait()
            if m < 2:
                value = jnp.dot(gath[where, :feat], (wg, wu)[m][:, at], preferred_element_type=f32)
            else:
                value = lax.dot_general(
                    gath[where, feat : 2 * feat], wd[at, :], NT, preferred_element_type=f32
                )
            part[m, where, at] = value
            sum_send[j, m, box] = part[m, part_rows(ch, 1 - y), at].astype(bf16)
        box = (j, slice(None), box)
        send(("sum", ch, j), sum_send.at[box], sum_recv.at[box], y_peer)

    gate_totals = {}

    def hidden_grads(ch, j):
        here, at, box = part_rows(ch, y), pl.ds(j * TILE, TILE), part_box(ch)
        arrived("sum", ch, j)
        gate, up, back = (part[m, here, at] + sum_recv[j, m, box].astype(f32) for m in range(3))
        sig = jax.nn.sigmoid(gate)
        act = gate * sig
        back_act = back * act
        total = jnp.sum(back_act * up, axis=1, keepdims=True)
        gate_totals[ch] = gate_totals[ch] + total if j else total
        grads[j, here, :TILE] = (back * up * sig * (1.0 + gate * (1.0 - sig))).astype(bf16)
        grads[j, here, TILE:] = back_act.astype(bf16)
        send(("grad", ch, j), grads.at[j, here], grads.at[j, here], y_peer)
        if j == tiles - 1:
            lanes = lax.broadcasted_iota(jnp.int32, (chunks[ch][1] * plane // 2, LANES), 1)
            gate_sums[here] = jnp.where(lanes == node, gate_totals[ch], 0.0).astype(bf16)
            send(("gates", ch), gate_sums.at[here], gate_sums.at[here], y_peer)

    def second_products(ch, picked, features):
        where, size = chunk_rows(ch), chunks[ch][1] * plane
        scale = None
        if picked[-1] == tiles - 1:
            lanes = lax.broadcasted_iota(jnp.int32, (size, LANES), 1)
            chosen = (lax.rem(lanes, experts) == node) & (lanes < 3 * experts)
            scale = jnp.sum(
                jnp.where(chosen, gath[where, 2 * feat :].astype(f32), 0.0), axis=1, keepdims=True
            )

        def feature_tile(i, carry):
            at = pl.ds(pl.multiple_of(i * TILE, TILE), TILE)
            value = pair[where, at] if picked[0] else jnp.zeros((size, TILE), f32)
            for j in picked:
                for m in range(2):
                    value = value + lax.dot_general(
                        grads[j, where, m * TILE : (m + 1) * TILE],
                        (wg, wu)[m][at, j * TILE : (j + 1) * TILE],
                        NT,
                        preferred_element_type=f32,
                    )
            pair[where, at] = value if scale is None else value * scale
            return carry

        lax.fori_loop(features[0] // TILE, features[1] // TILE, feature_tile, 0)

    def early_products(ch, j):
        arrived("grad", ch, j)
        second_products(ch, [j], (0, feat))

    def late_products(ch, h):
        where = chunk_rows(ch)
        picked = [tiles - 1] if ch == last else list(range(tiles))
        if h == 0:
            for j in picked:
                arrived("grad", ch, j)
        second_products(ch, picked, (h * feat // 2, (h + 1) * feat // 2))
        if h == 1:
            arrived("gates", ch)
            pair[where, feat:] = gate_sums[where].astype(f32)
        lo, hi = halves[h]
        for k in chunk_planes(ch):
            for x_ in range(2):
                rc_send[k, x_, :, lo:hi] = pair[block(k, x_, 1 - core), lo:hi].astype(bf16)
        box = (pl.ds(*chunks[ch]), slice(None), slice(None), pl.ds(lo, hi - lo))
        send(("core", ch, h), rc_send.at[box], rc_recv.at[box], sibling)

    def reduce_chip(ch, h):
        lo, hi = halves[h]
        arrived("core", ch, h)
        for k in chunk_planes(ch):
            value = pair[block(k, 1 - x, core), lo:hi] + rc_recv[k, 1 - x, :, lo:hi].astype(f32)
            rx_send[k, :, lo:hi] = value.astype(bf16)
        box = (pl.ds(*chunks[ch]), slice(None), pl.ds(lo, hi - lo))
        send(("across", ch, h), rx_send.at[box], rx_recv.at[box], x_peer)

    def reduce_plane(ch, h):
        lo, hi = halves[h]
        arrived("across", ch, h)
        for k in chunk_planes(ch):
            value = pair[block(k, x, core), lo:hi] + rc_recv[k, x, :, lo:hi].astype(f32)
            value = value + rx_recv[k, :, lo:hi].astype(f32)
            if k == 0:
                pair[mine, lo:hi] = value
            else:
                rz_send[k, :, lo:hi] = value.astype(bf16)
                box = (k, slice(None), pl.ds(lo, hi - lo))
                send(("home", k, h), rz_send.at[box], rz_recv.at[box], z_peers[k])

    def both(stage, ch):
        for h in range(2):
            stage(ch, h)

    gather_own()
    gather_plane(0)
    gather_column(1)
    for k in range(2, planes):
        send_far(k)
    for ch in range(last + 1):
        ahead = []
        if ch == 0 and last > 0:
            ahead = [(gather_plane, 1)]
        elif ch < last:
            ahead = [(gather_column, k) for k in chunk_planes(last)]
            ahead += [(gather_plane, k) for k in chunk_planes(last)]
        for j in range(tiles):
            first_products(ch, j)
            for stage, k in ahead[j : j + 1]:
                stage(k)
            if ch:
                hidden_grads(ch - 1, j)
        for stage, k in ahead[tiles:]:
            stage(k)
    pending = [(ch, h) for ch in range(last) for h in range(2)]
    for j in range(tiles):
        hidden_grads(last, j)
        for ch, h in pending[j : j + 1]:
            late_products(ch, h)
    for ch, h in pending[tiles:]:
        late_products(ch, h)
    for j in range(tiles - 1):
        early_products(last, j)
        if j < last:
            both(reduce_chip, j)
        if 1 <= j <= last:
            both(reduce_plane, j - 1)
    both(late_products, last)
    both(reduce_chip, last)
    both(reduce_plane, last)

    found = None
    for h, (lo, hi) in enumerate(halves):
        total = pair[mine, lo:hi]
        for k in range(1, planes):
            arrived("home", k, h)
            total = total + rz_recv[k, :, lo:hi].astype(f32)
        out[:, lo : min(hi, feat)] = total[:, : min(hi, feat) - lo].astype(bf16)
        found = total[:, hi - lo - LANES :]
    for j in range(top_count):
        value = jnp.sum(jnp.where(lane == ids[j], found, 0.0), axis=1, keepdims=True)
        line = jnp.sum(jnp.where(diagonal, value, 0.0), axis=0, keepdims=True)
        out_gates[j : j + 1, :] = line.astype(bf16)
    for copy in copies.values():
        copy.wait_send()


def dense_on_device(tokens, grad_out, gates, expert_ids, w_gate, w_up, w_down):
    planes = lax.axis_size("node") // 4
    rows, feat = tokens.shape
    hidden = w_gate.shape[2]
    bf16, f32 = jnp.bfloat16, jnp.float32
    wide, tiles = feat + LANES, hidden // TILE
    vmem, hbm = pl.BlockSpec(memory_space=pltpu.VMEM), pl.BlockSpec(memory_space=pl.ANY)
    grad_tokens, grad_gates_t = pl.pallas_call(
        functools.partial(dense_kernel, planes),
        out_shape=(
            jax.ShapeDtypeStruct((rows, feat), bf16),
            jax.ShapeDtypeStruct(expert_ids.shape[::-1], bf16),
        ),
        in_specs=[vmem] * 4 + [hbm] * 3,
        out_specs=(vmem, vmem),
        scratch_shapes=[
            pltpu.VMEM((feat, hidden), bf16),
            pltpu.VMEM((feat, hidden), bf16),
            pltpu.VMEM((hidden, feat), bf16),
            pltpu.VMEM((planes * 4 * rows, 2 * feat + LANES), bf16),
            pltpu.VMEM((3, planes * 4 * rows, hidden), f32),
            pltpu.VMEM((tiles, 3, planes * 2 * rows, TILE), bf16),
            pltpu.VMEM((tiles, 3, planes * 2 * rows, TILE), bf16),
            pltpu.VMEM((tiles, planes * 4 * rows, 2 * TILE), bf16),
            pltpu.VMEM((planes * 4 * rows, LANES), bf16),
            pltpu.VMEM((planes * 4 * rows, wide), f32),
            pltpu.VMEM((planes, 2, rows, wide), bf16),
            pltpu.VMEM((planes, 2, rows, wide), bf16),
            pltpu.VMEM((planes, rows, wide), bf16),
            pltpu.VMEM((planes, rows, wide), bf16),
            pltpu.VMEM((planes, rows, wide), bf16),
            pltpu.VMEM((planes, rows, wide), bf16),
            pltpu.SemaphoreType.DMA((3,)),
            pltpu.SemaphoreType.DMA((planes * (12 + tiles),)),
            pltpu.SemaphoreType.DMA((planes * (12 + tiles),)),
        ],
        compiler_params=pltpu.CompilerParams(
            collective_id=0, has_side_effects=True, vmem_limit_bytes=56 * 1024 * 1024
        ),
    )(tokens, grad_out, gates.T, expert_ids.T, w_gate, w_up, w_down)
    return grad_tokens, grad_gates_t.T


def local_grads(gate_pre, up_pre, back_pre, reduce_axis):
    sigmoid_gate = jax.nn.sigmoid(gate_pre)
    act = gate_pre * sigmoid_gate
    partial_gate = jnp.sum(act * up_pre * back_pre, axis=reduce_axis)
    grad_up = (back_pre * act).astype(jnp.bfloat16)
    grad_gate = (back_pre * up_pre * sigmoid_gate * (1.0 + gate_pre * (1.0 - sigmoid_gate))).astype(
        jnp.bfloat16
    )
    return (grad_gate, grad_up, partial_gate)


def on_device(tokens, grad_out, gates, expert_ids, w_gate, w_up, w_down):
    n_node = lax.axis_size("node")
    tok_rows, feature_cols = tokens.shape
    top_count = expert_ids.shape[1]
    capacity = min(tok_rows, max(2, 2 * tok_rows * top_count // n_node))
    planes = n_node // 4
    if capacity == tok_rows and n_node == 4 * planes and planes > 1 and planes & (planes - 1) == 0 and 3 * n_node <= LANES:
        return dense_on_device(tokens, grad_out, gates, expert_ids, w_gate, w_up, w_down)
    flat_ids = expert_ids.reshape(-1)
    onehot = (flat_ids[:, None] == jnp.arange(n_node, dtype=jnp.int32)[None, :]).astype(jnp.int32)
    slot_rank = jnp.sum(onehot * (jnp.cumsum(onehot, axis=0) - 1), axis=1)
    target = flat_ids * capacity + slot_rank
    placed = (target[:, None] == jnp.arange(n_node * capacity, dtype=jnp.int32)[None, :]).astype(
        jnp.bfloat16
    )
    paired = jnp.repeat(jnp.concatenate([tokens, grad_out], axis=1), top_count, axis=0)
    outgoing = lax.dot_general(
        placed, paired, (((0,), (0,)), ((), ())), preferred_element_type=jnp.float32
    )
    outgoing = outgoing.astype(jnp.bfloat16).reshape(n_node, capacity, 2 * feature_cols)
    gate_cols = w_gate[0]
    up_cols = w_up[0]
    down_rows = w_down[0]
    incoming = lax.all_to_all(outgoing, "node", split_axis=0, concat_axis=0, tiled=True)
    sources = incoming.shape[0]
    slot_count = incoming.shape[1]
    row_count = sources * slot_count
    flat_in = incoming.reshape(row_count, 2 * feature_cols)
    x_rows = flat_in[:, :feature_cols]
    dy_rows = flat_in[:, feature_cols:]
    gate_pre = lax.dot_general(
        gate_cols, x_rows, (((0,), (1,)), ((), ())), preferred_element_type=jnp.float32
    )
    up_pre = lax.dot_general(
        up_cols, x_rows, (((0,), (1,)), ((), ())), preferred_element_type=jnp.float32
    )
    back_pre = lax.dot_general(
        down_rows, dy_rows, (((1,), (1,)), ((), ())), preferred_element_type=jnp.float32
    )
    summed = lax.psum_scatter(
        jnp.concatenate([gate_pre, up_pre, back_pre], axis=1),
        "local",
        scatter_dimension=0,
        tiled=True,
    )
    grad_gate, grad_up, partial_gate = local_grads(
        summed[:, :row_count], summed[:, row_count : 2 * row_count], summed[:, 2 * row_count :], 0
    )
    running = lax.dot_general(
        lax.all_gather(grad_gate, "local", axis=0, tiled=True),
        gate_cols,
        (((0,), (1,)), ((), ())),
        preferred_element_type=jnp.float32,
    )
    result = running + lax.dot_general(
        lax.all_gather(grad_up, "local", axis=0, tiled=True),
        up_cols,
        (((0,), (1,)), ((), ())),
        preferred_element_type=jnp.float32,
    )
    gate_total = lax.psum(partial_gate, "local").astype(jnp.bfloat16)
    sent_rows = result.astype(jnp.bfloat16).reshape(sources, slot_count, feature_cols)
    sent_gates = gate_total.reshape(sources, slot_count)
    back_rows = lax.all_to_all(sent_rows, "node", split_axis=0, concat_axis=0, tiled=True)
    back_gates = lax.all_to_all(sent_gates, "node", split_axis=0, concat_axis=0, tiled=True)
    picked = jnp.take(back_rows.reshape(n_node * capacity, feature_cols), target, axis=0)
    picked = picked.reshape(tok_rows, top_count, feature_cols).astype(jnp.float32)
    grad_tokens = jnp.sum(picked * gates[:, :, None], axis=1).astype(jnp.bfloat16)
    grad_gates = jnp.take(back_gates.reshape(-1), target, axis=0).reshape(tok_rows, top_count)
    return (grad_tokens, grad_gates)


def solution(mesh):
    in_specs = (
        P("node", "local"),
        P("node", "local"),
        P("node", None),
        P("node", None),
        P("node", "local", None),
        P("node", "local", None),
        P("node", None, "local"),
    )
    out_specs = (P("node", "local"), P("node", None))
    return jax.shard_map(
        on_device, mesh=mesh, in_specs=in_specs, out_specs=out_specs, check_vma=False
    )
```

```python
import functools

import jax
import jax.numpy as jnp
from jax import lax
from jax.experimental import pallas as pl
from jax.experimental.pallas import tpu as pltpu
from jax.sharding import PartitionSpec as P

MESH = pl.DeviceIdType.MESH
LANES = 128
TILE = 256
NT = (((1,), (1,)), ((), ()))


def flipped(value, bits):
    place = 1
    while place <= bits:
        if bits & place:
            value = value + place * (1 - 2 * lax.rem(lax.div(value, place), 2))
        place *= 2
    return value


def dense_kernel(
    planes, tokens, grad_out, gates_t, ids_t, wg_hbm, wu_hbm, wd_hbm, out, out_gates,
    wg, wu, wd, gath, part, sum_send, sum_recv, grads, gate_sums, pair, rc_send, rc_recv,
    rx_send, rx_recv, rz_send, rz_recv, w_sem, send_sem, recv_sem,
):
    node, y = lax.axis_index("node"), lax.axis_index("local")
    core, x, z = lax.rem(node, 2), lax.rem(lax.div(node, 2), 2), lax.div(node, 4)
    rows, feat = tokens.shape
    hidden = wg.shape[1]
    experts = 4 * planes
    plane = 4 * rows
    tiles = hidden // TILE
    f32, bf16 = jnp.float32, jnp.bfloat16
    halves = ((0, feat // 2), (feat // 2, feat + LANES))

    def device(z_, x_, c_):
        return (z_ * 4 + x_ * 2 + c_, y)

    x_peer, sibling = device(z, 1 - x, core), device(z, x, 1 - core)
    y_peer = (node, 1 - y)
    z_peers = [None] + [device(flipped(z, k), x, core) for k in range(1, planes)]

    def block(k, x_, c_):
        return pl.ds(pl.multiple_of(k * plane + (x_ * 2 + c_) * rows, rows), rows)

    mine = block(0, x, core)
    chunks = [(0, 1)] + ([(1, 1)] if planes > 2 else []) + [(planes // 2, planes - planes // 2)]
    last = len(chunks) - 1

    def chunk_planes(ch):
        return range(chunks[ch][0], chunks[ch][0] + chunks[ch][1])

    def chunk_rows(ch):
        return pl.ds(chunks[ch][0] * plane, chunks[ch][1] * plane)

    def part_rows(ch, which):
        size = chunks[ch][1] * plane // 2
        return pl.ds(pl.multiple_of(chunks[ch][0] * plane + which * size, 2 * rows), size)

    def part_box(ch):
        return pl.ds(chunks[ch][0] * plane // 2, chunks[ch][1] * plane // 2)

    loads = [
        pltpu.make_async_copy(src.at[0], dst, w_sem.at[i])
        for i, (src, dst) in enumerate(((wg_hbm, wg), (wu_hbm, wu), (wd_hbm, wd)))
    ]
    for load in loads:
        load.start()

    barrier = pltpu.get_barrier_semaphore()
    peers = [x_peer, sibling, y_peer] + z_peers[1:]
    for peer in peers:
        pl.semaphore_signal(barrier, inc=1, device_id=peer, device_id_type=MESH)

    gath[mine, :feat] = tokens[...]
    gath[mine, feat : 2 * feat] = grad_out[...]
    lane = lax.broadcasted_iota(jnp.int32, (rows, LANES), 1)
    expert_lane = lax.rem(lane, experts)
    weight = jnp.zeros((rows, LANES), f32)
    top_count = ids_t.shape[0]
    diagonal = lax.broadcasted_iota(jnp.int32, (rows, rows), 0) == lax.broadcasted_iota(
        jnp.int32, (rows, rows), 1
    )

    def column(line):
        return jnp.sum(jnp.where(diagonal, line, 0.0), axis=1, keepdims=True)

    ids = [column(ids_t[j : j + 1, :].astype(f32)).astype(jnp.int32) for j in range(top_count)]
    for j in range(top_count):
        weight = weight + jnp.where(expert_lane == ids[j], column(gates_t[j : j + 1, :]), 0.0)
    top = weight.astype(bf16).astype(f32)
    middle = (weight - top).astype(bf16).astype(f32)
    low = weight - top - middle
    packed = jnp.where(
        lane < experts, top, jnp.where(lane < 2 * experts, middle, jnp.where(lane < 3 * experts, low, 0.0))
    )
    gath[mine, 2 * feat :] = packed.astype(bf16)

    pl.semaphore_wait(barrier, len(peers))

    copies = {}

    def send(name, src, dst, peer):
        i = len(copies)
        copies[name] = pltpu.make_async_remote_copy(
            src_ref=src, dst_ref=dst, send_sem=send_sem.at[i], recv_sem=recv_sem.at[i],
            device_id=peer, device_id_type=MESH,
        )
        copies[name].start()

    def arrived(*name):
        copies[name].wait_recv()

    def forward(name, where, peer):
        send(name, gath.at[where], gath.at[where], peer)

    def send_far(k):
        send(("z", k), gath.at[mine], gath.at[block(k, x, core)], z_peers[k])

    def gather_own():
        forward(("x", 0), mine, x_peer)
        forward(("a", 0), mine, sibling)
        for k in range(1, planes):
            send_far(k)

    def gather_column(k):
        arrived("z", k)
        forward(("x", k), block(k, x, core), x_peer)
        forward(("a", k), block(k, x, core), sibling)

    def gather_plane(k):
        arrived("x", k)
        forward(("b", k), block(k, 1 - x, core), sibling)

    def first_products(ch, j):
        where, at, box = chunk_rows(ch), pl.ds(j * TILE, TILE), part_box(ch)
        if j == 0:
            for k in chunk_planes(ch):
                arrived("a", k)
                arrived("b", k)
        for m in range(3):
            if ch == 0 and j == 0:
                loads[m].wait()
            if m < 2:
                value = jnp.dot(gath[where, :feat], (wg, wu)[m][:, at], preferred_element_type=f32)
            else:
                value = lax.dot_general(
                    gath[where, feat : 2 * feat], wd[at, :], NT, preferred_element_type=f32
                )
            part[m, where, at] = value
            sum_send[j, m, box] = part[m, part_rows(ch, 1 - y), at].astype(bf16)
        box = (j, slice(None), box)
        send(("sum", ch, j), sum_send.at[box], sum_recv.at[box], y_peer)

    gate_totals = {}

    def hidden_grads(ch, j):
        here, at, box = part_rows(ch, y), pl.ds(j * TILE, TILE), part_box(ch)
        arrived("sum", ch, j)
        gate, up, back = (part[m, here, at] + sum_recv[j, m, box].astype(f32) for m in range(3))
        sig = jax.nn.sigmoid(gate)
        act = gate * sig
        back_act = back * act
        total = jnp.sum(back_act * up, axis=1, keepdims=True)
        gate_totals[ch] = gate_totals[ch] + total if j else total
        grads[j, here, :TILE] = (back * up * sig * (1.0 + gate * (1.0 - sig))).astype(bf16)
        grads[j, here, TILE:] = back_act.astype(bf16)
        send(("grad", ch, j), grads.at[j, here], grads.at[j, here], y_peer)
        if j == tiles - 1:
            lanes = lax.broadcasted_iota(jnp.int32, (chunks[ch][1] * plane // 2, LANES), 1)
            gate_sums[here] = jnp.where(lanes == node, gate_totals[ch], 0.0).astype(bf16)
            send(("gates", ch), gate_sums.at[here], gate_sums.at[here], y_peer)

    def second_products(ch, picked, features):
        where, size = chunk_rows(ch), chunks[ch][1] * plane
        scale = None
        if picked[-1] == tiles - 1:
            lanes = lax.broadcasted_iota(jnp.int32, (size, LANES), 1)
            chosen = (lax.rem(lanes, experts) == node) & (lanes < 3 * experts)
            scale = jnp.sum(
                jnp.where(chosen, gath[where, 2 * feat :].astype(f32), 0.0), axis=1, keepdims=True
            )

        def feature_tile(i, carry):
            at = pl.ds(pl.multiple_of(i * TILE, TILE), TILE)
            value = pair[where, at] if picked[0] else jnp.zeros((size, TILE), f32)
            for j in picked:
                for m in range(2):
                    value = value + lax.dot_general(
                        grads[j, where, m * TILE : (m + 1) * TILE],
                        (wg, wu)[m][at, j * TILE : (j + 1) * TILE],
                        NT,
                        preferred_element_type=f32,
                    )
            pair[where, at] = value if scale is None else value * scale
            return carry

        lax.fori_loop(features[0] // TILE, features[1] // TILE, feature_tile, 0)

    def early_products(ch, j):
        arrived("grad", ch, j)
        second_products(ch, [j], (0, feat))

    def late_products(ch, h):
        where = chunk_rows(ch)
        picked = [tiles - 1] if ch == last else list(range(tiles))
        if h == 0:
            for j in picked:
                arrived("grad", ch, j)
        second_products(ch, picked, (h * feat // 2, (h + 1) * feat // 2))
        if h == 1:
            arrived("gates", ch)
            pair[where, feat:] = gate_sums[where].astype(f32)
        lo, hi = halves[h]
        for k in chunk_planes(ch):
            for x_ in range(2):
                rc_send[k, x_, :, lo:hi] = pair[block(k, x_, 1 - core), lo:hi].astype(bf16)
        box = (pl.ds(*chunks[ch]), slice(None), slice(None), pl.ds(lo, hi - lo))
        send(("core", ch, h), rc_send.at[box], rc_recv.at[box], sibling)

    def reduce_chip(ch, h):
        lo, hi = halves[h]
        arrived("core", ch, h)
        for k in chunk_planes(ch):
            value = pair[block(k, 1 - x, core), lo:hi] + rc_recv[k, 1 - x, :, lo:hi].astype(f32)
            rx_send[k, :, lo:hi] = value.astype(bf16)
        box = (pl.ds(*chunks[ch]), slice(None), pl.ds(lo, hi - lo))
        send(("across", ch, h), rx_send.at[box], rx_recv.at[box], x_peer)

    def reduce_plane(ch, h):
        lo, hi = halves[h]
        arrived("across", ch, h)
        for k in chunk_planes(ch):
            value = pair[block(k, x, core), lo:hi] + rc_recv[k, x, :, lo:hi].astype(f32)
            value = value + rx_recv[k, :, lo:hi].astype(f32)
            if k == 0:
                pair[mine, lo:hi] = value
            else:
                rz_send[k, :, lo:hi] = value.astype(bf16)
                box = (k, slice(None), pl.ds(lo, hi - lo))
                send(("home", k, h), rz_send.at[box], rz_recv.at[box], z_peers[k])

    def both(stage, ch):
        for h in range(2):
            stage(ch, h)

    gather_own()
    gather_plane(0)
    ahead = [[] for unused in range(tiles * (last + 1))]
    for k in range(1, planes):
        ahead[min(2 * k - 2 if k < 3 else k, tiles * last - 2)].append((gather_column, k))
        ahead[min(1 if k == 1 else 2 * k, tiles * last - 1)].append((gather_plane, k))
    for ch in range(last + 1):
        for j in range(tiles):
            first_products(ch, j)
            for stage, k in ahead[ch * tiles + j]:
                stage(k)
            if ch:
                hidden_grads(ch - 1, j)
    pending = [(ch, h) for ch in range(last) for h in range(2)]
    for j in range(tiles):
        hidden_grads(last, j)
        for ch, h in pending[j : j + 1]:
            late_products(ch, h)
    for ch, h in pending[tiles:]:
        late_products(ch, h)
    for j in range(tiles - 1):
        early_products(last, j)
        if j < last:
            both(reduce_chip, j)
        if 1 <= j <= last:
            both(reduce_plane, j - 1)
    both(late_products, last)
    both(reduce_chip, last)
    both(reduce_plane, last)

    found = None
    for h, (lo, hi) in enumerate(halves):
        total = pair[mine, lo:hi]
        for k in range(1, planes):
            arrived("home", k, h)
            total = total + rz_recv[k, :, lo:hi].astype(f32)
        out[:, lo : min(hi, feat)] = total[:, : min(hi, feat) - lo].astype(bf16)
        found = total[:, hi - lo - LANES :]
    for j in range(top_count):
        value = jnp.sum(jnp.where(lane == ids[j], found, 0.0), axis=1, keepdims=True)
        line = jnp.sum(jnp.where(diagonal, value, 0.0), axis=0, keepdims=True)
        out_gates[j : j + 1, :] = line.astype(bf16)
    for copy in copies.values():
        copy.wait_send()


def dense_on_device(tokens, grad_out, gates, expert_ids, w_gate, w_up, w_down):
    planes = lax.axis_size("node") // 4
    rows, feat = tokens.shape
    hidden = w_gate.shape[2]
    bf16, f32 = jnp.bfloat16, jnp.float32
    wide, tiles = feat + LANES, hidden // TILE
    vmem, hbm = pl.BlockSpec(memory_space=pltpu.VMEM), pl.BlockSpec(memory_space=pl.ANY)
    grad_tokens, grad_gates_t = pl.pallas_call(
        functools.partial(dense_kernel, planes),
        out_shape=(
            jax.ShapeDtypeStruct((rows, feat), bf16),
            jax.ShapeDtypeStruct(expert_ids.shape[::-1], bf16),
        ),
        in_specs=[vmem] * 4 + [hbm] * 3,
        out_specs=(vmem, vmem),
        scratch_shapes=[
            pltpu.VMEM((feat, hidden), bf16),
            pltpu.VMEM((feat, hidden), bf16),
            pltpu.VMEM((hidden, feat), bf16),
            pltpu.VMEM((planes * 4 * rows, 2 * feat + LANES), bf16),
            pltpu.VMEM((3, planes * 4 * rows, hidden), f32),
            pltpu.VMEM((tiles, 3, planes * 2 * rows, TILE), bf16),
            pltpu.VMEM((tiles, 3, planes * 2 * rows, TILE), bf16),
            pltpu.VMEM((tiles, planes * 4 * rows, 2 * TILE), bf16),
            pltpu.VMEM((planes * 4 * rows, LANES), bf16),
            pltpu.VMEM((planes * 4 * rows, wide), f32),
            pltpu.VMEM((planes, 2, rows, wide), bf16),
            pltpu.VMEM((planes, 2, rows, wide), bf16),
            pltpu.VMEM((planes, rows, wide), bf16),
            pltpu.VMEM((planes, rows, wide), bf16),
            pltpu.VMEM((planes, rows, wide), bf16),
            pltpu.VMEM((planes, rows, wide), bf16),
            pltpu.SemaphoreType.DMA((3,)),
            pltpu.SemaphoreType.DMA((planes * (12 + tiles),)),
            pltpu.SemaphoreType.DMA((planes * (12 + tiles),)),
        ],
        compiler_params=pltpu.CompilerParams(
            collective_id=0, has_side_effects=True, vmem_limit_bytes=56 * 1024 * 1024
        ),
    )(tokens, grad_out, gates.T, expert_ids.T, w_gate, w_up, w_down)
    return grad_tokens, grad_gates_t.T


def local_grads(gate_pre, up_pre, back_pre, reduce_axis):
    sigmoid_gate = jax.nn.sigmoid(gate_pre)
    act = gate_pre * sigmoid_gate
    partial_gate = jnp.sum(act * up_pre * back_pre, axis=reduce_axis)
    grad_up = (back_pre * act).astype(jnp.bfloat16)
    grad_gate = (back_pre * up_pre * sigmoid_gate * (1.0 + gate_pre * (1.0 - sigmoid_gate))).astype(
        jnp.bfloat16
    )
    return (grad_gate, grad_up, partial_gate)


def on_device(tokens, grad_out, gates, expert_ids, w_gate, w_up, w_down):
    n_node = lax.axis_size("node")
    tok_rows, feature_cols = tokens.shape
    top_count = expert_ids.shape[1]
    capacity = min(tok_rows, max(2, 2 * tok_rows * top_count // n_node))
    planes = n_node // 4
    if capacity == tok_rows and n_node == 4 * planes and planes > 1 and planes & (planes - 1) == 0 and 3 * n_node <= LANES:
        return dense_on_device(tokens, grad_out, gates, expert_ids, w_gate, w_up, w_down)
    flat_ids = expert_ids.reshape(-1)
    onehot = (flat_ids[:, None] == jnp.arange(n_node, dtype=jnp.int32)[None, :]).astype(jnp.int32)
    slot_rank = jnp.sum(onehot * (jnp.cumsum(onehot, axis=0) - 1), axis=1)
    target = flat_ids * capacity + slot_rank
    placed = (target[:, None] == jnp.arange(n_node * capacity, dtype=jnp.int32)[None, :]).astype(
        jnp.bfloat16
    )
    paired = jnp.repeat(jnp.concatenate([tokens, grad_out], axis=1), top_count, axis=0)
    outgoing = lax.dot_general(
        placed, paired, (((0,), (0,)), ((), ())), preferred_element_type=jnp.float32
    )
    outgoing = outgoing.astype(jnp.bfloat16).reshape(n_node, capacity, 2 * feature_cols)
    gate_cols = w_gate[0]
    up_cols = w_up[0]
    down_rows = w_down[0]
    incoming = lax.all_to_all(outgoing, "node", split_axis=0, concat_axis=0, tiled=True)
    sources = incoming.shape[0]
    slot_count = incoming.shape[1]
    row_count = sources * slot_count
    flat_in = incoming.reshape(row_count, 2 * feature_cols)
    x_rows = flat_in[:, :feature_cols]
    dy_rows = flat_in[:, feature_cols:]
    gate_pre = lax.dot_general(
        gate_cols, x_rows, (((0,), (1,)), ((), ())), preferred_element_type=jnp.float32
    )
    up_pre = lax.dot_general(
        up_cols, x_rows, (((0,), (1,)), ((), ())), preferred_element_type=jnp.float32
    )
    back_pre = lax.dot_general(
        down_rows, dy_rows, (((1,), (1,)), ((), ())), preferred_element_type=jnp.float32
    )
    summed = lax.psum_scatter(
        jnp.concatenate([gate_pre, up_pre, back_pre], axis=1),
        "local",
        scatter_dimension=0,
        tiled=True,
    )
    grad_gate, grad_up, partial_gate = local_grads(
        summed[:, :row_count], summed[:, row_count : 2 * row_count], summed[:, 2 * row_count :], 0
    )
    running = lax.dot_general(
        lax.all_gather(grad_gate, "local", axis=0, tiled=True),
        gate_cols,
        (((0,), (1,)), ((), ())),
        preferred_element_type=jnp.float32,
    )
    result = running + lax.dot_general(
        lax.all_gather(grad_up, "local", axis=0, tiled=True),
        up_cols,
        (((0,), (1,)), ((), ())),
        preferred_element_type=jnp.float32,
    )
    gate_total = lax.psum(partial_gate, "local").astype(jnp.bfloat16)
    sent_rows = result.astype(jnp.bfloat16).reshape(sources, slot_count, feature_cols)
    sent_gates = gate_total.reshape(sources, slot_count)
    back_rows = lax.all_to_all(sent_rows, "node", split_axis=0, concat_axis=0, tiled=True)
    back_gates = lax.all_to_all(sent_gates, "node", split_axis=0, concat_axis=0, tiled=True)
    picked = jnp.take(back_rows.reshape(n_node * capacity, feature_cols), target, axis=0)
    picked = picked.reshape(tok_rows, top_count, feature_cols).astype(jnp.float32)
    grad_tokens = jnp.sum(picked * gates[:, :, None], axis=1).astype(jnp.bfloat16)
    grad_gates = jnp.take(back_gates.reshape(-1), target, axis=0).reshape(tok_rows, top_count)
    return (grad_tokens, grad_gates)


def solution(mesh):
    in_specs = (
        P("node", "local"),
        P("node", "local"),
        P("node", None),
        P("node", None),
        P("node", "local", None),
        P("node", "local", None),
        P("node", None, "local"),
    )
    out_specs = (P("node", "local"), P("node", None))
    return jax.shard_map(
        on_device, mesh=mesh, in_specs=in_specs, out_specs=out_specs, check_vma=False
    )
```

```python
import functools

import jax
import jax.numpy as jnp
from jax import lax
from jax.experimental import pallas as pl
from jax.experimental.pallas import tpu as pltpu
from jax.sharding import PartitionSpec as P

MESH = pl.DeviceIdType.MESH
LANES = 128
TILE = 256
AG_Z, AG_X, AG_A, AG_B, SUM_Y, GRAD_Y, RS_C, RS_X, RS_Z, KINDS = 0, 1, 2, 3, 4, 7, 8, 9, 10, 11
NT = (((1,), (1,)), ((), ()))


def flipped(value, bits):
    place = 1
    while place <= bits:
        if bits & place:
            value = value + place * (1 - 2 * lax.rem(lax.div(value, place), 2))
        place *= 2
    return value


def dense_kernel(
    planes, tokens, grad_out, gates_t, ids_t, wg_hbm, wu_hbm, wd_hbm, out, out_gates,
    wg, wu, wd, gath, part, sum_send, sum_recv, grads, pair, rc_send, rc_recv,
    rx_send, rx_recv, rz_send, rz_recv, w_sem, send_sem, recv_sem,
):
    node, y = lax.axis_index("node"), lax.axis_index("local")
    core, x, z = lax.rem(node, 2), lax.rem(lax.div(node, 2), 2), lax.div(node, 4)
    rows, feat = tokens.shape
    hidden = wg.shape[1]
    experts = 4 * planes
    half = 2 * rows
    f32, bf16 = jnp.float32, jnp.bfloat16

    def device(z_, x_, c_):
        return (z_ * 4 + x_ * 2 + c_, y)

    x_peer, sibling = device(z, 1 - x, core), device(z, x, 1 - core)
    y_peer = (node, 1 - y)
    z_peers = [None] + [device(flipped(z, k), x, core) for k in range(1, planes)]

    def block(x_, c_, size=rows):
        return pl.ds(pl.multiple_of((x_ * 2 + c_) * rows, rows), size)

    mine, here = block(x, core), block(y, 0, half)
    theirs = block(1 - y, 0, half)

    loads = [
        pltpu.make_async_copy(src.at[0], dst, w_sem.at[i])
        for i, (src, dst) in enumerate(((wg_hbm, wg), (wu_hbm, wu), (wd_hbm, wd)))
    ]
    for load in loads:
        load.start()

    barrier = pltpu.get_barrier_semaphore()
    peers = [x_peer, sibling, y_peer] + z_peers[1:]
    for peer in peers:
        pl.semaphore_signal(barrier, inc=1, device_id=peer, device_id_type=MESH)

    gath[0, mine, :feat] = tokens[...]
    gath[0, mine, feat : 2 * feat] = grad_out[...]
    lane = lax.broadcasted_iota(jnp.int32, (rows, LANES), 1)
    expert_lane = lax.rem(lane, experts)
    weight = jnp.zeros((rows, LANES), f32)
    top_count = ids_t.shape[0]
    diagonal = lax.broadcasted_iota(jnp.int32, (rows, rows), 0) == lax.broadcasted_iota(
        jnp.int32, (rows, rows), 1
    )

    def column(line):
        return jnp.sum(jnp.where(diagonal, line, 0.0), axis=1, keepdims=True)

    ids = [column(ids_t[j : j + 1, :].astype(f32)).astype(jnp.int32) for j in range(top_count)]
    for j in range(top_count):
        weight = weight + jnp.where(expert_lane == ids[j], column(gates_t[j : j + 1, :]), 0.0)
    top = weight.astype(bf16).astype(f32)
    middle = (weight - top).astype(bf16).astype(f32)
    low = weight - top - middle
    packed = jnp.where(
        lane < experts, top, jnp.where(lane < 2 * experts, middle, jnp.where(lane < 3 * experts, low, 0.0))
    )
    gath[0, mine, 2 * feat :] = packed.astype(bf16)

    pl.semaphore_wait(barrier, len(peers))

    copies = {}

    def send(kind, k, src, dst, peer):
        copies[kind, k] = pltpu.make_async_remote_copy(
            src_ref=src, dst_ref=dst, send_sem=send_sem.at[k, kind], recv_sem=recv_sem.at[k, kind],
            device_id=peer, device_id_type=MESH,
        )
        copies[kind, k].start()

    def arrived(kind, k):
        copies[kind, k].wait_recv()

    def forward(kind, k, where, peer):
        send(kind, k, gath.at[k, where], gath.at[k, where], peer)

    def gather_column(k):
        if k:
            arrived(AG_Z, k)
        forward(AG_X, k, mine, x_peer)
        if k == 0:
            for far in range(1, planes):
                send(AG_Z, far, gath.at[0, mine], gath.at[far, mine], z_peers[far])
        forward(AG_A, k, mine, sibling)

    def gather_plane(k):
        arrived(AG_X, k)
        forward(AG_B, k, block(1 - x, core), sibling)

    def first_products(k):
        arrived(AG_A, k)
        arrived(AG_B, k)
        for m in range(3):
            if k == 0:
                loads[m].wait()

            def column_tile(j, carry, m=m):
                at = pl.ds(pl.multiple_of(j * TILE, TILE), TILE)
                if m < 2:
                    value = jnp.dot(gath[k, :, :feat], (wg, wu)[m][:, at], preferred_element_type=f32)
                else:
                    value = lax.dot_general(
                        gath[k, :, feat : 2 * feat], wd[at, :], NT, preferred_element_type=f32
                    )
                part[k, m, :, at] = value
                return carry

            lax.fori_loop(0, hidden // TILE, column_tile, 0)
            sum_send[k, m] = part[k, m, theirs, :].astype(bf16)
            send(SUM_Y + m, k, sum_send.at[k, m], sum_recv.at[k, m], y_peer)

    def hidden_grads(k):
        for m in range(3):
            arrived(SUM_Y + m, k)
        total = jnp.zeros((half, 1), f32)
        for j in range(hidden // TILE):
            at = pl.ds(j * TILE, TILE)
            gate, up, back = (
                part[k, m, here, at] + sum_recv[k, m, :, at].astype(f32) for m in range(3)
            )
            sig = jax.nn.sigmoid(gate)
            act = gate * sig
            back_act = back * act
            total = total + jnp.sum(back_act * up, axis=1, keepdims=True)
            grads[k, here, j * TILE : (j + 1) * TILE] = (
                back * up * sig * (1.0 + gate * (1.0 - sig))
            ).astype(bf16)
            grads[k, here, hidden + j * TILE : hidden + (j + 1) * TILE] = back_act.astype(bf16)
        lanes = lax.broadcasted_iota(jnp.int32, (half, LANES), 1)
        grads[k, here, 2 * hidden :] = jnp.where(lanes == node, total, 0.0).astype(bf16)
        send(GRAD_Y, k, grads.at[k, here], grads.at[k, here], y_peer)

    def second_products(k):
        arrived(GRAD_Y, k)
        lanes = lax.broadcasted_iota(jnp.int32, (2 * half, LANES), 1)
        chosen = (lax.rem(lanes, experts) == node) & (lanes < 3 * experts)
        scale = jnp.sum(
            jnp.where(chosen, gath[k, :, 2 * feat :].astype(f32), 0.0), axis=1, keepdims=True
        )

        def feature_tile(j, carry):
            at = pl.ds(pl.multiple_of(j * TILE, TILE), TILE)
            value = lax.dot_general(grads[k, :, :hidden], wg[at, :], NT, preferred_element_type=f32)
            value = value + lax.dot_general(
                grads[k, :, hidden : 2 * hidden], wu[at, :], NT, preferred_element_type=f32
            )
            pair[k, :, at] = value * scale
            return carry

        lax.fori_loop(0, feat // TILE, feature_tile, 0)
        pair[k, :, feat:] = grads[k, :, 2 * hidden :].astype(f32)
        for x_ in range(2):
            rc_send[k, x_] = pair[k, block(x_, 1 - core), :].astype(bf16)
        send(RS_C, k, rc_send.at[k], rc_recv.at[k], sibling)

    def chip_sum(k, x_):
        return pair[k, block(x_, core), :] + rc_recv[k, x_].astype(f32)

    def reduce_chip(k):
        arrived(RS_C, k)
        rx_send[k] = chip_sum(k, 1 - x).astype(bf16)
        send(RS_X, k, rx_send.at[k], rx_recv.at[k], x_peer)

    def reduce_plane(k):
        arrived(RS_X, k)
        value = chip_sum(k, x) + rx_recv[k].astype(f32)
        if k == 0:
            pair[0, mine, :] = value
        else:
            rz_send[k] = value.astype(bf16)
            send(RS_Z, k, rz_send.at[k], rz_recv.at[k], z_peers[k])

    stages = (
        (gather_column, 0), (gather_plane, 1), (first_products, 1), (reduce_chip, 4),
        (hidden_grads, 2), (second_products, 3), (reduce_plane, 5),
    )
    for turn in range(planes + 5):
        for stage, lag in stages:
            if 0 <= turn - lag < planes:
                stage(turn - lag)

    total = pair[0, mine, :]
    for k in range(1, planes):
        arrived(RS_Z, k)
        total = total + rz_recv[k].astype(f32)
    out[...] = total[:, :feat].astype(bf16)
    found = total[:, feat:]
    for j in range(top_count):
        value = jnp.sum(jnp.where(lane == ids[j], found, 0.0), axis=1, keepdims=True)
        line = jnp.sum(jnp.where(diagonal, value, 0.0), axis=0, keepdims=True)
        out_gates[j : j + 1, :] = line.astype(bf16)
    for copy in copies.values():
        copy.wait_send()


def dense_on_device(tokens, grad_out, gates, expert_ids, w_gate, w_up, w_down):
    planes = lax.axis_size("node") // 4
    rows, feat = tokens.shape
    hidden = w_gate.shape[2]
    bf16, f32 = jnp.bfloat16, jnp.float32
    wide = feat + LANES
    vmem, hbm = pl.BlockSpec(memory_space=pltpu.VMEM), pl.BlockSpec(memory_space=pl.ANY)
    grad_tokens, grad_gates_t = pl.pallas_call(
        functools.partial(dense_kernel, planes),
        out_shape=(
            jax.ShapeDtypeStruct((rows, feat), bf16),
            jax.ShapeDtypeStruct(expert_ids.shape[::-1], bf16),
        ),
        in_specs=[vmem] * 4 + [hbm] * 3,
        out_specs=(vmem, vmem),
        scratch_shapes=[
            pltpu.VMEM((feat, hidden), bf16),
            pltpu.VMEM((feat, hidden), bf16),
            pltpu.VMEM((hidden, feat), bf16),
            pltpu.VMEM((planes, 4 * rows, 2 * feat + LANES), bf16),
            pltpu.VMEM((planes, 3, 4 * rows, hidden), f32),
            pltpu.VMEM((planes, 3, 2 * rows, hidden), bf16),
            pltpu.VMEM((planes, 3, 2 * rows, hidden), bf16),
            pltpu.VMEM((planes, 4 * rows, 2 * hidden + LANES), bf16),
            pltpu.VMEM((planes, 4 * rows, wide), f32),
            pltpu.VMEM((planes, 2, rows, wide), bf16),
            pltpu.VMEM((planes, 2, rows, wide), bf16),
            pltpu.VMEM((planes, rows, wide), bf16),
            pltpu.VMEM((planes, rows, wide), bf16),
            pltpu.VMEM((planes, rows, wide), bf16),
            pltpu.VMEM((planes, rows, wide), bf16),
            pltpu.SemaphoreType.DMA((3,)),
            pltpu.SemaphoreType.DMA((planes, KINDS)),
            pltpu.SemaphoreType.DMA((planes, KINDS)),
        ],
        compiler_params=pltpu.CompilerParams(
            collective_id=0, has_side_effects=True, vmem_limit_bytes=56 * 1024 * 1024
        ),
    )(tokens, grad_out, gates.T, expert_ids.T, w_gate, w_up, w_down)
    return grad_tokens, grad_gates_t.T


def local_grads(gate_pre, up_pre, back_pre, reduce_axis):
    sigmoid_gate = jax.nn.sigmoid(gate_pre)
    act = gate_pre * sigmoid_gate
    partial_gate = jnp.sum(act * up_pre * back_pre, axis=reduce_axis)
    grad_up = (back_pre * act).astype(jnp.bfloat16)
    grad_gate = (back_pre * up_pre * sigmoid_gate * (1.0 + gate_pre * (1.0 - sigmoid_gate))).astype(
        jnp.bfloat16
    )
    return (grad_gate, grad_up, partial_gate)


def on_device(tokens, grad_out, gates, expert_ids, w_gate, w_up, w_down):
    n_node = lax.axis_size("node")
    tok_rows, feature_cols = tokens.shape
    top_count = expert_ids.shape[1]
    capacity = min(tok_rows, max(2, 2 * tok_rows * top_count // n_node))
    planes = n_node // 4
    if capacity == tok_rows and n_node == 4 * planes and planes & (planes - 1) == 0 and 3 * n_node <= LANES:
        return dense_on_device(tokens, grad_out, gates, expert_ids, w_gate, w_up, w_down)
    flat_ids = expert_ids.reshape(-1)
    onehot = (flat_ids[:, None] == jnp.arange(n_node, dtype=jnp.int32)[None, :]).astype(jnp.int32)
    slot_rank = jnp.sum(onehot * (jnp.cumsum(onehot, axis=0) - 1), axis=1)
    target = flat_ids * capacity + slot_rank
    placed = (target[:, None] == jnp.arange(n_node * capacity, dtype=jnp.int32)[None, :]).astype(
        jnp.bfloat16
    )
    paired = jnp.repeat(jnp.concatenate([tokens, grad_out], axis=1), top_count, axis=0)
    outgoing = lax.dot_general(
        placed, paired, (((0,), (0,)), ((), ())), preferred_element_type=jnp.float32
    )
    outgoing = outgoing.astype(jnp.bfloat16).reshape(n_node, capacity, 2 * feature_cols)
    gate_cols = w_gate[0]
    up_cols = w_up[0]
    down_rows = w_down[0]
    incoming = lax.all_to_all(outgoing, "node", split_axis=0, concat_axis=0, tiled=True)
    sources = incoming.shape[0]
    slot_count = incoming.shape[1]
    row_count = sources * slot_count
    flat_in = incoming.reshape(row_count, 2 * feature_cols)
    x_rows = flat_in[:, :feature_cols]
    dy_rows = flat_in[:, feature_cols:]
    gate_pre = lax.dot_general(
        gate_cols, x_rows, (((0,), (1,)), ((), ())), preferred_element_type=jnp.float32
    )
    up_pre = lax.dot_general(
        up_cols, x_rows, (((0,), (1,)), ((), ())), preferred_element_type=jnp.float32
    )
    back_pre = lax.dot_general(
        down_rows, dy_rows, (((1,), (1,)), ((), ())), preferred_element_type=jnp.float32
    )
    summed = lax.psum_scatter(
        jnp.concatenate([gate_pre, up_pre, back_pre], axis=1),
        "local",
        scatter_dimension=0,
        tiled=True,
    )
    grad_gate, grad_up, partial_gate = local_grads(
        summed[:, :row_count], summed[:, row_count : 2 * row_count], summed[:, 2 * row_count :], 0
    )
    running = lax.dot_general(
        lax.all_gather(grad_gate, "local", axis=0, tiled=True),
        gate_cols,
        (((0,), (1,)), ((), ())),
        preferred_element_type=jnp.float32,
    )
    result = running + lax.dot_general(
        lax.all_gather(grad_up, "local", axis=0, tiled=True),
        up_cols,
        (((0,), (1,)), ((), ())),
        preferred_element_type=jnp.float32,
    )
    gate_total = lax.psum(partial_gate, "local").astype(jnp.bfloat16)
    sent_rows = result.astype(jnp.bfloat16).reshape(sources, slot_count, feature_cols)
    sent_gates = gate_total.reshape(sources, slot_count)
    back_rows = lax.all_to_all(sent_rows, "node", split_axis=0, concat_axis=0, tiled=True)
    back_gates = lax.all_to_all(sent_gates, "node", split_axis=0, concat_axis=0, tiled=True)
    picked = jnp.take(back_rows.reshape(n_node * capacity, feature_cols), target, axis=0)
    picked = picked.reshape(tok_rows, top_count, feature_cols).astype(jnp.float32)
    grad_tokens = jnp.sum(picked * gates[:, :, None], axis=1).astype(jnp.bfloat16)
    grad_gates = jnp.take(back_gates.reshape(-1), target, axis=0).reshape(tok_rows, top_count)
    return (grad_tokens, grad_gates)


def solution(mesh):
    in_specs = (
        P("node", "local"),
        P("node", "local"),
        P("node", None),
        P("node", None),
        P("node", "local", None),
        P("node", "local", None),
        P("node", None, "local"),
    )
    out_specs = (P("node", "local"), P("node", None))
    return jax.shard_map(
        on_device, mesh=mesh, in_specs=in_specs, out_specs=out_specs, check_vma=False
    )
```

```python
import functools

import jax
import jax.numpy as jnp
from jax import lax
from jax.experimental import pallas as pl
from jax.experimental.pallas import tpu as pltpu
from jax.sharding import PartitionSpec as P

MESH = pl.DeviceIdType.MESH
LANES = 128
TILE = 512
AG_Z, AG_X, AG_A, AG_B, SUM_Y, GRAD_Y, RS_C, RS_X, RS_Z, KINDS = 0, 1, 2, 3, 4, 7, 8, 9, 10, 11
NT = (((1,), (1,)), ((), ()))


def flipped(value, bits):
    place = 1
    while place <= bits:
        if bits & place:
            value = value + place * (1 - 2 * lax.rem(lax.div(value, place), 2))
        place *= 2
    return value


def dense_kernel(
    planes, tokens, grad_out, gates_t, ids_t, wg_hbm, wu_hbm, wd_hbm, out, out_gates,
    wg, wu, wd, gath, part, sum_send, sum_recv, grads, pair, rc_send, rc_recv,
    rx_send, rx_recv, rz_send, rz_recv, w_sem, send_sem, recv_sem,
):
    node, y = lax.axis_index("node"), lax.axis_index("local")
    core, x, z = lax.rem(node, 2), lax.rem(lax.div(node, 2), 2), lax.div(node, 4)
    rows, feat = tokens.shape
    hidden = wg.shape[1]
    experts = 4 * planes
    half = 2 * rows
    f32, bf16 = jnp.float32, jnp.bfloat16

    def device(z_, x_, c_):
        return (z_ * 4 + x_ * 2 + c_, y)

    x_peer, sibling = device(z, 1 - x, core), device(z, x, 1 - core)
    y_peer = (node, 1 - y)
    z_peers = [None] + [device(flipped(z, k), x, core) for k in range(1, planes)]

    def block(x_, c_, size=rows):
        return pl.ds(pl.multiple_of((x_ * 2 + c_) * rows, rows), size)

    mine, here = block(x, core), block(y, 0, half)
    theirs = block(1 - y, 0, half)

    loads = [
        pltpu.make_async_copy(src.at[0], dst, w_sem.at[i])
        for i, (src, dst) in enumerate(((wg_hbm, wg), (wu_hbm, wu), (wd_hbm, wd)))
    ]
    for load in loads:
        load.start()

    barrier = pltpu.get_barrier_semaphore()
    peers = [x_peer, sibling, y_peer] + z_peers[1:]
    for peer in peers:
        pl.semaphore_signal(barrier, inc=1, device_id=peer, device_id_type=MESH)

    gath[0, mine, :feat] = tokens[...]
    gath[0, mine, feat : 2 * feat] = grad_out[...]
    lane = lax.broadcasted_iota(jnp.int32, (rows, LANES), 1)
    expert_lane = lax.rem(lane, experts)
    weight = jnp.zeros((rows, LANES), f32)
    top_count = ids_t.shape[0]
    diagonal = lax.broadcasted_iota(jnp.int32, (rows, rows), 0) == lax.broadcasted_iota(
        jnp.int32, (rows, rows), 1
    )

    def column(line):
        return jnp.sum(jnp.where(diagonal, line, 0.0), axis=1, keepdims=True)

    ids = [column(ids_t[j : j + 1, :].astype(f32)).astype(jnp.int32) for j in range(top_count)]
    for j in range(top_count):
        weight = weight + jnp.where(expert_lane == ids[j], column(gates_t[j : j + 1, :]), 0.0)
    top = weight.astype(bf16).astype(f32)
    middle = (weight - top).astype(bf16).astype(f32)
    low = weight - top - middle
    packed = jnp.where(
        lane < experts, top, jnp.where(lane < 2 * experts, middle, jnp.where(lane < 3 * experts, low, 0.0))
    )
    gath[0, mine, 2 * feat :] = packed.astype(bf16)

    pl.semaphore_wait(barrier, len(peers))

    copies = {}

    def send(kind, k, src, dst, peer):
        copies[kind, k] = pltpu.make_async_remote_copy(
            src_ref=src, dst_ref=dst, send_sem=send_sem.at[k, kind], recv_sem=recv_sem.at[k, kind],
            device_id=peer, device_id_type=MESH,
        )
        copies[kind, k].start()

    def arrived(kind, k):
        copies[kind, k].wait_recv()

    def forward(kind, k, where, peer):
        send(kind, k, gath.at[k, where], gath.at[k, where], peer)

    def gather_column(k):
        if k:
            arrived(AG_Z, k)
        forward(AG_X, k, mine, x_peer)
        if k == 0:
            for far in range(1, planes):
                send(AG_Z, far, gath.at[0, mine], gath.at[far, mine], z_peers[far])
        forward(AG_A, k, mine, sibling)

    def gather_plane(k):
        arrived(AG_X, k)
        forward(AG_B, k, block(1 - x, core), sibling)

    def first_products(k):
        arrived(AG_A, k)
        arrived(AG_B, k)
        for m in range(3):
            if k == 0:
                loads[m].wait()

            def column_tile(j, carry, m=m):
                at = pl.ds(pl.multiple_of(j * TILE, TILE), TILE)
                if m < 2:
                    value = jnp.dot(gath[k, :, :feat], (wg, wu)[m][:, at], preferred_element_type=f32)
                else:
                    value = lax.dot_general(
                        gath[k, :, feat : 2 * feat], wd[at, :], NT, preferred_element_type=f32
                    )
                part[k, m, :, at] = value
                return carry

            lax.fori_loop(0, hidden // TILE, column_tile, 0)
            sum_send[k, m] = part[k, m, theirs, :].astype(bf16)
            send(SUM_Y + m, k, sum_send.at[k, m], sum_recv.at[k, m], y_peer)

    def hidden_grads(k):
        for m in range(3):
            arrived(SUM_Y + m, k)
        total = jnp.zeros((half, 1), f32)
        for j in range(hidden // TILE):
            at = pl.ds(j * TILE, TILE)
            gate, up, back = (
                part[k, m, here, at] + sum_recv[k, m, :, at].astype(f32) for m in range(3)
            )
            sig = jax.nn.sigmoid(gate)
            act = gate * sig
            back_act = back * act
            total = total + jnp.sum(back_act * up, axis=1, keepdims=True)
            grads[k, here, j * TILE : (j + 1) * TILE] = (
                back * up * sig * (1.0 + gate * (1.0 - sig))
            ).astype(bf16)
            grads[k, here, hidden + j * TILE : hidden + (j + 1) * TILE] = back_act.astype(bf16)
        lanes = lax.broadcasted_iota(jnp.int32, (half, LANES), 1)
        grads[k, here, 2 * hidden :] = jnp.where(lanes == node, total, 0.0).astype(bf16)
        send(GRAD_Y, k, grads.at[k, here], grads.at[k, here], y_peer)

    def second_products(k):
        arrived(GRAD_Y, k)
        lanes = lax.broadcasted_iota(jnp.int32, (2 * half, LANES), 1)
        chosen = (lax.rem(lanes, experts) == node) & (lanes < 3 * experts)
        scale = jnp.sum(
            jnp.where(chosen, gath[k, :, 2 * feat :].astype(f32), 0.0), axis=1, keepdims=True
        )

        def feature_tile(j, carry):
            at = pl.ds(pl.multiple_of(j * TILE, TILE), TILE)
            value = lax.dot_general(grads[k, :, :hidden], wg[at, :], NT, preferred_element_type=f32)
            value = value + lax.dot_general(
                grads[k, :, hidden : 2 * hidden], wu[at, :], NT, preferred_element_type=f32
            )
            pair[k, :, at] = value * scale
            return carry

        lax.fori_loop(0, feat // TILE, feature_tile, 0)
        pair[k, :, feat:] = grads[k, :, 2 * hidden :].astype(f32)
        for x_ in range(2):
            rc_send[k, x_] = pair[k, block(x_, 1 - core), :].astype(bf16)
        send(RS_C, k, rc_send.at[k], rc_recv.at[k], sibling)

    def chip_sum(k, x_):
        return pair[k, block(x_, core), :] + rc_recv[k, x_].astype(f32)

    def reduce_chip(k):
        arrived(RS_C, k)
        rx_send[k] = chip_sum(k, 1 - x).astype(bf16)
        send(RS_X, k, rx_send.at[k], rx_recv.at[k], x_peer)

    def reduce_plane(k):
        arrived(RS_X, k)
        value = chip_sum(k, x) + rx_recv[k].astype(f32)
        if k == 0:
            pair[0, mine, :] = value
        else:
            rz_send[k] = value.astype(bf16)
            send(RS_Z, k, rz_send.at[k], rz_recv.at[k], z_peers[k])

    stages = (
        (gather_column, 0), (gather_plane, 1), (first_products, 1), (reduce_chip, 4),
        (hidden_grads, 2), (second_products, 3), (reduce_plane, 5),
    )
    for turn in range(planes + 5):
        for stage, lag in stages:
            if 0 <= turn - lag < planes:
                stage(turn - lag)

    total = pair[0, mine, :]
    for k in range(1, planes):
        arrived(RS_Z, k)
        total = total + rz_recv[k].astype(f32)
    out[...] = total[:, :feat].astype(bf16)
    found = total[:, feat:]
    for j in range(top_count):
        value = jnp.sum(jnp.where(lane == ids[j], found, 0.0), axis=1, keepdims=True)
        line = jnp.sum(jnp.where(diagonal, value, 0.0), axis=0, keepdims=True)
        out_gates[j : j + 1, :] = line.astype(bf16)
    for copy in copies.values():
        copy.wait_send()


def dense_on_device(tokens, grad_out, gates, expert_ids, w_gate, w_up, w_down):
    planes = lax.axis_size("node") // 4
    rows, feat = tokens.shape
    hidden = w_gate.shape[2]
    bf16, f32 = jnp.bfloat16, jnp.float32
    wide = feat + LANES
    vmem, hbm = pl.BlockSpec(memory_space=pltpu.VMEM), pl.BlockSpec(memory_space=pl.ANY)
    grad_tokens, grad_gates_t = pl.pallas_call(
        functools.partial(dense_kernel, planes),
        out_shape=(
            jax.ShapeDtypeStruct((rows, feat), bf16),
            jax.ShapeDtypeStruct(expert_ids.shape[::-1], bf16),
        ),
        in_specs=[vmem] * 4 + [hbm] * 3,
        out_specs=(vmem, vmem),
        scratch_shapes=[
            pltpu.VMEM((feat, hidden), bf16),
            pltpu.VMEM((feat, hidden), bf16),
            pltpu.VMEM((hidden, feat), bf16),
            pltpu.VMEM((planes, 4 * rows, 2 * feat + LANES), bf16),
            pltpu.VMEM((planes, 3, 4 * rows, hidden), f32),
            pltpu.VMEM((planes, 3, 2 * rows, hidden), bf16),
            pltpu.VMEM((planes, 3, 2 * rows, hidden), bf16),
            pltpu.VMEM((planes, 4 * rows, 2 * hidden + LANES), bf16),
            pltpu.VMEM((planes, 4 * rows, wide), f32),
            pltpu.VMEM((planes, 2, rows, wide), bf16),
            pltpu.VMEM((planes, 2, rows, wide), bf16),
            pltpu.VMEM((planes, rows, wide), bf16),
            pltpu.VMEM((planes, rows, wide), bf16),
            pltpu.VMEM((planes, rows, wide), bf16),
            pltpu.VMEM((planes, rows, wide), bf16),
            pltpu.SemaphoreType.DMA((3,)),
            pltpu.SemaphoreType.DMA((planes, KINDS)),
            pltpu.SemaphoreType.DMA((planes, KINDS)),
        ],
        compiler_params=pltpu.CompilerParams(
            collective_id=0, has_side_effects=True, vmem_limit_bytes=56 * 1024 * 1024
        ),
    )(tokens, grad_out, gates.T, expert_ids.T, w_gate, w_up, w_down)
    return grad_tokens, grad_gates_t.T


def local_grads(gate_pre, up_pre, back_pre, reduce_axis):
    sigmoid_gate = jax.nn.sigmoid(gate_pre)
    act = gate_pre * sigmoid_gate
    partial_gate = jnp.sum(act * up_pre * back_pre, axis=reduce_axis)
    grad_up = (back_pre * act).astype(jnp.bfloat16)
    grad_gate = (back_pre * up_pre * sigmoid_gate * (1.0 + gate_pre * (1.0 - sigmoid_gate))).astype(
        jnp.bfloat16
    )
    return (grad_gate, grad_up, partial_gate)


def on_device(tokens, grad_out, gates, expert_ids, w_gate, w_up, w_down):
    n_node = lax.axis_size("node")
    tok_rows, feature_cols = tokens.shape
    top_count = expert_ids.shape[1]
    capacity = min(tok_rows, max(2, 2 * tok_rows * top_count // n_node))
    planes = n_node // 4
    if capacity == tok_rows and n_node == 4 * planes and planes & (planes - 1) == 0 and 3 * n_node <= LANES:
        return dense_on_device(tokens, grad_out, gates, expert_ids, w_gate, w_up, w_down)
    flat_ids = expert_ids.reshape(-1)
    onehot = (flat_ids[:, None] == jnp.arange(n_node, dtype=jnp.int32)[None, :]).astype(jnp.int32)
    slot_rank = jnp.sum(onehot * (jnp.cumsum(onehot, axis=0) - 1), axis=1)
    target = flat_ids * capacity + slot_rank
    placed = (target[:, None] == jnp.arange(n_node * capacity, dtype=jnp.int32)[None, :]).astype(
        jnp.bfloat16
    )
    paired = jnp.repeat(jnp.concatenate([tokens, grad_out], axis=1), top_count, axis=0)
    outgoing = lax.dot_general(
        placed, paired, (((0,), (0,)), ((), ())), preferred_element_type=jnp.float32
    )
    outgoing = outgoing.astype(jnp.bfloat16).reshape(n_node, capacity, 2 * feature_cols)
    gate_cols = w_gate[0]
    up_cols = w_up[0]
    down_rows = w_down[0]
    incoming = lax.all_to_all(outgoing, "node", split_axis=0, concat_axis=0, tiled=True)
    sources = incoming.shape[0]
    slot_count = incoming.shape[1]
    row_count = sources * slot_count
    flat_in = incoming.reshape(row_count, 2 * feature_cols)
    x_rows = flat_in[:, :feature_cols]
    dy_rows = flat_in[:, feature_cols:]
    gate_pre = lax.dot_general(
        gate_cols, x_rows, (((0,), (1,)), ((), ())), preferred_element_type=jnp.float32
    )
    up_pre = lax.dot_general(
        up_cols, x_rows, (((0,), (1,)), ((), ())), preferred_element_type=jnp.float32
    )
    back_pre = lax.dot_general(
        down_rows, dy_rows, (((1,), (1,)), ((), ())), preferred_element_type=jnp.float32
    )
    summed = lax.psum_scatter(
        jnp.concatenate([gate_pre, up_pre, back_pre], axis=1),
        "local",
        scatter_dimension=0,
        tiled=True,
    )
    grad_gate, grad_up, partial_gate = local_grads(
        summed[:, :row_count], summed[:, row_count : 2 * row_count], summed[:, 2 * row_count :], 0
    )
    running = lax.dot_general(
        lax.all_gather(grad_gate, "local", axis=0, tiled=True),
        gate_cols,
        (((0,), (1,)), ((), ())),
        preferred_element_type=jnp.float32,
    )
    result = running + lax.dot_general(
        lax.all_gather(grad_up, "local", axis=0, tiled=True),
        up_cols,
        (((0,), (1,)), ((), ())),
        preferred_element_type=jnp.float32,
    )
    gate_total = lax.psum(partial_gate, "local").astype(jnp.bfloat16)
    sent_rows = result.astype(jnp.bfloat16).reshape(sources, slot_count, feature_cols)
    sent_gates = gate_total.reshape(sources, slot_count)
    back_rows = lax.all_to_all(sent_rows, "node", split_axis=0, concat_axis=0, tiled=True)
    back_gates = lax.all_to_all(sent_gates, "node", split_axis=0, concat_axis=0, tiled=True)
    picked = jnp.take(back_rows.reshape(n_node * capacity, feature_cols), target, axis=0)
    picked = picked.reshape(tok_rows, top_count, feature_cols).astype(jnp.float32)
    grad_tokens = jnp.sum(picked * gates[:, :, None], axis=1).astype(jnp.bfloat16)
    grad_gates = jnp.take(back_gates.reshape(-1), target, axis=0).reshape(tok_rows, top_count)
    return (grad_tokens, grad_gates)


def solution(mesh):
    in_specs = (
        P("node", "local"),
        P("node", "local"),
        P("node", None),
        P("node", None),
        P("node", "local", None),
        P("node", "local", None),
        P("node", None, "local"),
    )
    out_specs = (P("node", "local"), P("node", None))
    return jax.shard_map(
        on_device, mesh=mesh, in_specs=in_specs, out_specs=out_specs, check_vma=False
    )
```
